32 devices in a mesh: section: 4 (over y, core), ctx: 2 (over x), mp: 4 (over z).
Axes of the slice: x: 2, y: 2, z: 4, core: 2. Of those that a mesh axis runs over, the one named last changes fastest.
Arguments:
- query_rows: bfloat16 [4, 512, 4096], P('section', 'ctx', 'mp'), may hold values from -6 to 6
- key_rows: bfloat16 [4, 512, 4096], P('section', 'ctx', 'mp'), may hold values from -6 to 6
- value_rows: bfloat16 [4, 512, 4096], P('section', 'ctx', 'mp'), may hold values from -6 to 6
- long_filter: bfloat16 [4, 512, 4096], P('section', 'ctx', 'mp'), may hold values from -1.1 to 1.1, as said below
- short_filter: float32 [4, 3, 3, 4096], P('section', None, None, 'mp'), may hold values from -3 to 3
- next_weight: bfloat16 [4, 4096, 4096], P('section', 'mp', 'ctx'), may hold values from -0.09375 to 0.09375
Outputs:
- projected: bfloat16 [4, 512, 4096], P('section', 'ctx', 'mp')
The draws below stay inside these ranges and needn't reach their ends.
Inputs may be any that keep to these rules, and one draw needn't show every extreme that they name: `long_filter`: the filter's entries shrink with the lag at a per-channel rate.
All inputs are finite; a program needn't handle non-finite values.
Results may differ from the reference program's by a relative error of at most 0.0051.
Values may be sent and summed in bfloat16 or wider, within the bound.
No kernel may reach another device: no remote copies, remote signals or barrier semaphores. Data moves between devices by JAX's collectives and lax.ppermute only.
A program may use at most 128 MiB of HBM per device.

```python
import math
import jax
import jax.numpy as jnp

D = 4096
SHORT = 3
TOKENS = 512
SECTIONS = 4


def draw_long_filter(key, part):
    key = jax.random.fold_in(key, 11)
    rate_key, noise_key = jax.random.split(key)
    low_rate = 1.0 / TOKENS
    high_rate = 1.0 / 30.0
    noise = jnp.clip(jax.random.normal(noise_key, (SECTIONS, TOKENS, D), jnp.float32), -4.0, 4.0)
    rate = jnp.exp(jax.random.uniform(rate_key, (SECTIONS, 1, D), jnp.float32, math.log(low_rate), math.log(high_rate)))
    lag = jnp.arange(TOKENS, dtype=jnp.float32)[None, :, None]
    scale = jnp.sqrt((1.0 - jnp.exp(-2.0 * rate)) / (1.0 - jnp.exp(-2.0 * rate * TOKENS)))
    return (noise * jnp.exp(-rate * lag) * scale).astype(jnp.bfloat16)


def shard_levels(own_key, dims, pieces, least, high):
    def one(position, parts):
        heights = jax.random.uniform(jax.random.fold_in(jax.random.fold_in(own_key, 6), position), (parts,), jnp.float32, least / len(pieces), high / len(pieces))
        return jnp.repeat(jnp.exp(heights), dims[position] // parts).reshape((-1,) + (1,) * (len(dims) - position - 1))

    gain = one(*pieces[0])
    for cut in pieces[1:]:
        gain = gain * one(*cut)
    return gain


def gaussian(rng, extent, width, limit, pieces=(), held_as=jnp.bfloat16):
    result = jax.random.normal(rng, extent, jnp.float32) * width
    if len(pieces) > 0:
        result = shard_levels(rng, extent, pieces, -0.22, 0.18) * result
    return jnp.clip(result, min=-limit, max=limit).astype(held_as)


def setup_inputs(seed: int = 0) -> dict:
    arg_keys = jax.random.split(jax.random.key(seed), 7)
    query_rows = gaussian(arg_keys[0], (SECTIONS, TOKENS, D), 1.0, 6.0, ((0, 4), (1, 2), (2, 4)))
    key_rows = gaussian(arg_keys[1], (SECTIONS, TOKENS, D), 1.0, 6.0, ((0, 4), (1, 2), (2, 4)))
    value_rows = gaussian(arg_keys[2], (SECTIONS, TOKENS, D), 1.0, 6.0, ((0, 4), (1, 2), (2, 4)))
    long_filter = draw_long_filter(jax.random.fold_in(arg_keys[6], 71), 0)
    short_filter = gaussian(arg_keys[4], (SECTIONS, 3, SHORT, D), 0.6, 3.0, ((0, 4), (3, 4)), jnp.float32)
    next_weight = gaussian(arg_keys[5], (SECTIONS, D, D), D ** -0.5, 0.09375, ((0, 4), (1, 4), (2, 2)))
    return {"query_rows": query_rows, "key_rows": key_rows, "value_rows": value_rows, "long_filter": long_filter, "short_filter": short_filter, "next_weight": next_weight}


def short_conv(rows, taps):
    padded = jnp.pad(rows.astype(jnp.float32), ((2, 0), (0, 0)))
    return taps[0] * padded[2:] + taps[1] * padded[1:-1] + taps[2] * padded[:-2]


def hyena_layer(query, key_branch, value_branch, filter_rows, taps):
    query_feat = short_conv(query, taps[0])
    key_feat = short_conv(key_branch, taps[1])
    value_feat = short_conv(value_branch, taps[2])
    mixed_input = key_feat * value_feat
    length_padded = 2 * TOKENS
    spectrum = jnp.fft.rfft(mixed_input, n=length_padded, axis=0) * jnp.fft.rfft(filter_rows.astype(jnp.float32), n=length_padded, axis=0)
    convolved = jnp.fft.irfft(spectrum, n=length_padded, axis=0)[:TOKENS]
    return (query_feat * convolved).astype(jnp.bfloat16)


def reference(query_rows, key_rows, value_rows, long_filter, short_filter, next_weight):
    outputs = [hyena_layer(query_rows[index], key_rows[index], value_rows[index], long_filter[index], short_filter[index]) for index in range(SECTIONS)]
    results = []
    for index in range(SECTIONS):
        source = outputs[(index - 1) % SECTIONS]
        results.append(jnp.dot(source, next_weight[index], preferred_element_type=jnp.float32).astype(jnp.bfloat16))
    return jnp.stack(results)
```

```python
import functools
import math

import jax
import jax.numpy as jnp
import ml_dtypes
import numpy as np
from jax import lax
from jax.experimental import pallas as pl
from jax.experimental.pallas import tpu as pltpu
from jax.sharding import PartitionSpec as P

F32 = jnp.float32
BF16 = jnp.bfloat16
EXTRA = 16
VMEM_LIMIT = 56 * 2**20


def odd_tables(length):
    k = np.arange(length, dtype=np.int64)[:, None]
    n = np.arange(length, dtype=np.int64)[None, :]
    turn = ((2 * k + 1) * n) % (4 * length)
    angle = turn.astype(np.float64) * (math.pi / (2 * length))
    forward = np.concatenate([np.cos(angle), np.sin(angle)], axis=0)
    high = forward.astype(ml_dtypes.bfloat16)
    low = (forward - high.astype(np.float64)).astype(ml_dtypes.bfloat16)
    scale = np.float64(1.0 / length)
    back = forward.T * scale
    back_high = back.astype(ml_dtypes.bfloat16)
    back_low = (back - back_high.astype(np.float64)).astype(ml_dtypes.bfloat16)
    return high, low, back_high, back_low


def down(rows, by):
    index = lax.broadcasted_iota(jnp.int32, rows.shape, 0)
    return jnp.where(index >= by, pltpu.roll(rows, by, 0), 0.0)


def short_filtered(rows, taps):
    return taps[0:1] * rows + taps[1:2] * down(rows, 1) + taps[2:3] * down(rows, 2)


def mix_kernel(place, key_ref, value_ref, taps_ref, send_ref, own_ref):
    rows, width = own_ref.shape[0] - EXTRA, own_ref.shape[1]
    for out_ref, half in ((send_ref, 1 - place[0]), (own_ref, place[0])):
        lanes = pl.ds(pl.multiple_of(half * width, width), width)
        key = key_ref[:, lanes].astype(F32)
        value = value_ref[:, lanes].astype(F32)
        mixed = short_filtered(key, taps_ref[1, :, lanes]) * short_filtered(value, taps_ref[2, :, lanes])
        out_ref[:rows, :] = mixed.astype(BF16)
        edges = [key[:2], key[rows - 2 :], value[:2], value[rows - 2 :], jnp.zeros((EXTRA - 8, width), F32)]
        out_ref[rows:, :] = jnp.concatenate(edges, axis=0).astype(BF16)


def filter_kernel(place, own_ref, come_ref, high_ref, low_ref, spec_ref, whole):
    rows = own_ref.shape[0]
    whole[pl.ds(pl.multiple_of(place[0] * rows, rows), rows), :] = own_ref[...]
    whole[pl.ds(pl.multiple_of((1 - place[0]) * rows, rows), rows), :] = come_ref[...]
    data = whole[...]
    spec_ref[...] = jnp.dot(high_ref[...], data, preferred_element_type=F32) + jnp.dot(
        low_ref[...], data, preferred_element_type=F32
    )


def conv_kernel(
    place, own_ref, come_ref, taps_ref, spec_ref, high_ref, low_ref, back_high_ref, back_low_ref, out_ref, whole
):
    rows = own_ref.shape[0] - EXTRA
    first = place[0] == 0
    whole[pl.ds(pl.multiple_of(place[0] * rows, rows), rows), :] = own_ref[:rows, :]
    whole[pl.ds(pl.multiple_of((1 - place[0]) * rows, rows), rows), :] = come_ref[:rows, :]
    own_edge = own_ref[rows:, :].astype(F32)
    come_edge = come_ref[rows:, :].astype(F32)
    before = jnp.where(first, own_edge, come_edge)
    after = jnp.where(first, come_edge, own_edge)

    def edge_features(branch, base):
        taps = taps_ref[branch]
        older, old = before[base + 2 : base + 3], before[base + 3 : base + 4]
        new, newer = after[base : base + 1], after[base + 1 : base + 2]
        return (
            taps[0:1] * new + taps[1:2] * old + taps[2:3] * older,
            taps[0:1] * newer + taps[1:2] * new + taps[2:3] * old,
        )

    key_0, key_1 = edge_features(1, 0)
    value_0, value_1 = edge_features(2, 4)
    tile = whole[rows : rows + EXTRA, :].astype(F32)
    index = lax.broadcasted_iota(jnp.int32, tile.shape, 0)
    tile = jnp.where(index == 0, key_0 * value_0, jnp.where(index == 1, key_1 * value_1, tile))
    whole[rows : rows + EXTRA, :] = tile.astype(BF16)

    data = whole[...]
    half = high_ref.shape[0] // 2
    spec = jnp.dot(high_ref[...], data, preferred_element_type=F32) + jnp.dot(
        low_ref[...], data, preferred_element_type=F32
    )
    cos_a, sin_a = spec[:half], spec[half:]
    cos_b, sin_b = spec_ref[:half, :], spec_ref[half:, :]
    product = jnp.concatenate([cos_a * cos_b - sin_a * sin_b, cos_a * sin_b + sin_a * cos_b], axis=0)
    product_high = product.astype(BF16)
    product_low = (product - product_high.astype(F32)).astype(BF16)
    out_ref[...] = (
        jnp.dot(back_high_ref[...], product_high, preferred_element_type=F32)
        + jnp.dot(back_low_ref[...], product_high, preferred_element_type=F32)
        + jnp.dot(back_high_ref[...], product_low, preferred_element_type=F32)
    )


def gate_kernel(place, own_ref, come_ref, taps_ref, conv_ref, out_ref, whole):
    rows = own_ref.shape[0]
    whole[pl.ds(pl.multiple_of(place[0] * rows, rows), rows), :] = own_ref[...].astype(F32)
    whole[pl.ds(pl.multiple_of((1 - place[0]) * rows, rows), rows), :] = come_ref[...].astype(F32)
    out_ref[...] = (short_filtered(whole[...], taps_ref[0]) * conv_ref[...]).astype(BF16)


def project_kernel(place, same_ref, cross_ref, weight_ref, other_ref, own_ref):
    rows, depth = own_ref.shape[0], same_ref.shape[1]
    here, there = place[0], 1 - place[0]
    weight_same = weight_ref[pl.ds(pl.multiple_of(here * depth, depth), depth), :]
    weight_cross = weight_ref[pl.ds(pl.multiple_of(there * depth, depth), depth), :]
    for out_ref, which in ((other_ref, there), (own_ref, here)):
        tokens = pl.ds(pl.multiple_of(which * rows, rows), rows)
        out_ref[...] = (
            jnp.dot(same_ref[tokens, :], weight_same, preferred_element_type=F32)
            + jnp.dot(cross_ref[tokens, :], weight_cross, preferred_element_type=F32)
        ).astype(out_ref.dtype)


def params():
    return pltpu.CompilerParams(vmem_limit_bytes=VMEM_LIMIT)


def cost(flops, bytes_accessed):
    return pl.CostEstimate(flops=int(flops), bytes_accessed=int(bytes_accessed), transcendentals=0)


def shape(dims, dtype):
    return jax.ShapeDtypeStruct(dims, dtype)


def two_by_four(query_rows, key_rows, value_rows, long_filter, short_filter, next_weight):
    sections = lax.axis_size("section")
    query, key, value, filt = query_rows[0], key_rows[0], value_rows[0], long_filter[0]
    taps, weight = short_filter[0], next_weight[0]
    rows, channels = query.shape
    width = channels // 2
    length = 2 * rows
    columns = weight.shape[1] // 2
    x = lax.axis_index("ctx")
    z = lax.axis_index("mp")
    parity = z % 2
    place = jnp.stack([x, parity]).astype(jnp.int32)
    high, low, back_high, back_low = (jnp.asarray(t) for t in odd_tables(length))

    swap = [(0, 1), (1, 0)]

    def other_half(array):
        return lax.dynamic_slice_in_dim(array, (1 - x) * width, width, axis=1)

    filt_come = lax.ppermute(other_half(filt), "ctx", swap)
    mixed_send, mixed_own = pl.pallas_call(
        mix_kernel,
        grid_spec=pltpu.PrefetchScalarGridSpec(
            num_scalar_prefetch=1,
            grid=(1,),
            in_specs=[
                pl.BlockSpec((rows, channels), lambda i, p: (0, 0)),
                pl.BlockSpec((rows, channels), lambda i, p: (0, 0)),
                pl.BlockSpec((3, 3, channels), lambda i, p: (0, 0, 0)),
            ],
            out_specs=[pl.BlockSpec((rows + EXTRA, width), lambda i, p: (0, 0))] * 2,
        ),
        out_shape=[shape((rows + EXTRA, width), BF16)] * 2,
        compiler_params=params(),
        cost_estimate=cost(rows * channels * 20, rows * channels * 6),
    )(place, key, value, taps)
    mixed_come = lax.ppermute(mixed_send, "ctx", swap)
    query_come = lax.ppermute(other_half(query), "ctx", swap)

    block = min(256, width)
    steps = width // block

    own_lanes = pl.BlockSpec((rows, block), lambda i, p: (0, p[0] * steps + i))
    lanes = lambda n: pl.BlockSpec((n, block), lambda i, p: (0, i))
    taps_lanes = pl.BlockSpec((3, 3, block), lambda i, p: (0, 0, p[0] * steps + i))
    whole = lambda table: pl.BlockSpec(table.shape, lambda i, p: (0, 0))

    spectrum = pl.pallas_call(
        filter_kernel,
        grid_spec=pltpu.PrefetchScalarGridSpec(
            num_scalar_prefetch=1,
            grid=(steps,),
            in_specs=[own_lanes, lanes(rows), whole(high), whole(low)],
            out_specs=lanes(2 * length),
            scratch_shapes=[pltpu.VMEM((length, block), BF16)],
        ),
        out_shape=shape((2 * length, width), F32),
        compiler_params=params(),
        cost_estimate=cost(8 * length * length * width, 8 * length * length + 10 * length * width),
    )(place, filt, filt_come, high, low)
    convolved = pl.pallas_call(
        conv_kernel,
        grid_spec=pltpu.PrefetchScalarGridSpec(
            num_scalar_prefetch=1,
            grid=(steps,),
            in_specs=[
                lanes(rows + EXTRA),
                lanes(rows + EXTRA),
                taps_lanes,
                lanes(2 * length),
                whole(high),
                whole(low),
                whole(back_high),
                whole(back_low),
            ],
            out_specs=lanes(length),
            scratch_shapes=[pltpu.VMEM((length, block), BF16)],
        ),
        out_shape=shape((length, width), F32),
        compiler_params=params(),
        cost_estimate=cost(20 * length * length * width, 16 * length * length + 14 * length * width),
    )(place, mixed_own, mixed_come, taps, spectrum, high, low, back_high, back_low)
    hyena = pl.pallas_call(
        gate_kernel,
        grid_spec=pltpu.PrefetchScalarGridSpec(
            num_scalar_prefetch=1,
            grid=(steps,),
            in_specs=[own_lanes, lanes(rows), taps_lanes, lanes(length)],
            out_specs=lanes(length),
            scratch_shapes=[pltpu.VMEM((length, block), F32)],
        ),
        out_shape=shape((length, width), BF16),
        compiler_params=params(),
        cost_estimate=cost(10 * length * width, 8 * length * width),
    )(place, query, query_come, taps, convolved)

    def to_next(array, flip):
        pairs = [
            (s * 2 + c, (s + 1) % sections * 2 + (c + flip) % 2) for s in range(sections) for c in range(2)
        ]
        return lax.ppermute(array, ("section", "ctx"), pairs)

    cross = to_next(hyena, 1)
    same = to_next(hyena, 0)

    tile = min(256, columns)
    tiles = columns // tile

    def project(flip, own_dtype):
        pick = lambda p: (p[1] + flip) % 2
        return pl.pallas_call(
            project_kernel,
            grid_spec=pltpu.PrefetchScalarGridSpec(
                num_scalar_prefetch=1,
                grid=(tiles,),
                in_specs=[
                    pl.BlockSpec((length, width), lambda i, p: (0, 0)),
                    pl.BlockSpec((length, width), lambda i, p: (0, 0)),
                    pl.BlockSpec((channels, tile), lambda i, p: (0, pick(p) * tiles + i)),
                ],
                out_specs=[pl.BlockSpec((rows, tile), lambda i, p: (0, i))] * 2,
            ),
            out_shape=[shape((rows, columns), BF16), shape((rows, columns), own_dtype)],
            compiler_params=params(),
            cost_estimate=cost(2 * length * channels * columns, 2 * channels * (columns + length) + 2 * length * columns),
        )(place, same, cross, weight)

    near = [(i, i ^ 1) for i in range(4)]
    far = [(i, i ^ 2) for i in range(4)]
    cross_pass, own_pass = project(1, BF16)
    behind_pass = lax.ppermute(cross_pass, "ctx", swap)
    own_near = lax.ppermute(own_pass, "mp", near)
    cross_keep, own_keep = project(0, F32)
    behind_keep = lax.ppermute(cross_keep, "ctx", swap)
    behind_near = lax.ppermute(behind_pass, "mp", near)
    own_sum = own_keep + own_near.astype(F32)
    behind_sum = behind_keep.astype(F32) + behind_near.astype(F32)
    at_home = (z // 2) == x
    leaving = jnp.where(at_home, behind_sum, own_sum).astype(BF16)
    arriving = lax.ppermute(leaving, "mp", far)
    staying = jnp.where(at_home, own_sum, behind_sum)
    return (staying + arriving.astype(F32)).astype(BF16)[None]


def from_behind(value, axis, by):
    count = lax.axis_size(axis)
    pairs = [(i, i + by) for i in range(count) if 0 <= i + by < count]
    return lax.ppermute(value, axis, pairs)


def from_behind_2(value, axis, by):
    count = lax.axis_size(axis)
    return lax.ppermute(value, axis, [(i, (i + by) % count) for i in range(count)])


def phase_table(left, right, modulus):
    product = left[:, None] * right[None, :] % modulus
    angle = product.astype(jnp.float32) * (2.0 * math.pi / modulus)
    return (jnp.cos(angle), jnp.sin(angle))


def contract(pattern, table, data):
    return jnp.einsum(pattern, table, data, precision=lax.Precision.HIGHEST)


def rotate(cos_tab, sin_tab, orient, pattern, real_part, imag_part):
    new_real = contract(pattern, cos_tab, real_part) - orient * contract(
        pattern, sin_tab, imag_part
    )
    new_imag = contract(pattern, cos_tab, imag_part) + orient * contract(
        pattern, sin_tab, real_part
    )
    return (new_real, new_imag)


def transform(real_part, imag_part, orient):
    length = real_part.shape[-2]
    outer_len = math.gcd(length, 2 ** ((length.bit_length() - 1) // 2))
    inner_len = length // outer_len
    leading = real_part.shape[:-2]
    channels = real_part.shape[-1]
    real_part = real_part.reshape(leading + (outer_len, inner_len, channels))
    imag_part = imag_part.reshape(leading + (outer_len, inner_len, channels))
    outer_ids = jnp.arange(outer_len, dtype=jnp.int32)
    inner_ids = jnp.arange(inner_len, dtype=jnp.int32)
    cos_outer, sin_outer = phase_table(outer_ids, outer_ids, outer_len)
    real_part, imag_part = rotate(
        cos_outer, sin_outer, orient, "kn,...nbc->...kbc", real_part, imag_part
    )
    cos_twist, sin_twist = phase_table(outer_ids, inner_ids, length)
    cos_twist = cos_twist[:, :, None]
    sin_twist = sin_twist[:, :, None]
    real_part, imag_part = (
        real_part * cos_twist - orient * imag_part * sin_twist,
        imag_part * cos_twist + orient * real_part * sin_twist,
    )
    cos_inner, sin_inner = phase_table(inner_ids, inner_ids, inner_len)
    real_part, imag_part = rotate(
        cos_inner, sin_inner, orient, "qb,...kbc->...qkc", real_part, imag_part
    )
    return (
        real_part.reshape(leading + (length, channels)),
        imag_part.reshape(leading + (length, channels)),
    )


def any_mesh(query_rows, key_rows, value_rows, long_filter, short_filter, next_weight):
    blocks = lax.axis_size("ctx")
    query_local = query_rows[0]
    key_local = key_rows[0]
    value_local = value_rows[0]
    tok_dev = query_local.shape[0]
    total = 2 * tok_dev * blocks
    stacked = jnp.stack([query_local[-2:], key_local[-2:], value_local[-2:]])
    carried = from_behind(stacked, "ctx", 1)
    taps = short_filter[0]

    def featurize(branch, current):
        extended = jnp.concatenate([carried[branch], current], axis=0).astype(jnp.float32)
        return (
            taps[branch, 0] * extended[2:]
            + taps[branch, 1] * extended[1:-1]
            + taps[branch, 2] * extended[:-2]
        )

    query_feat = featurize(0, query_local)
    mixed_input = featurize(1, key_local) * featurize(2, value_local)
    pair = jnp.stack([mixed_input, long_filter[0].astype(jnp.float32)])
    whole = lax.all_to_all(pair, "ctx", split_axis=2, concat_axis=1, tiled=True)
    padded = jnp.concatenate([whole, jnp.zeros_like(whole)], axis=1)
    spec_real, spec_imag = transform(padded, jnp.zeros_like(padded), -1.0)
    prod_real = spec_real[0] * spec_real[1] - spec_imag[0] * spec_imag[1]
    prod_imag = spec_real[0] * spec_imag[1] + spec_imag[0] * spec_real[1]
    conv_real, conv_imag = transform(prod_real, prod_imag, 1.0)
    values_out = conv_real[: tok_dev * blocks] / total
    convolved = lax.all_to_all(values_out, "ctx", split_axis=0, concat_axis=1, tiled=True)
    hyena_out = (query_feat * convolved).astype(jnp.bfloat16)
    incoming = from_behind_2(hyena_out, "section", 1)
    weight_local = next_weight[0]
    partial_value = jnp.dot(
        incoming,
        lax.all_gather(weight_local, "ctx", axis=1, tiled=True),
        preferred_element_type=jnp.float32,
    )
    summed = lax.psum_scatter(partial_value, "mp", scatter_dimension=1, tiled=True)
    return summed.astype(jnp.bfloat16)[None]


def solution(mesh):
    in_specs = (
        P("section", "ctx", "mp"),
        P("section", "ctx", "mp"),
        P("section", "ctx", "mp"),
        P("section", "ctx", "mp"),
        P("section", None, None, "mp"),
        P("section", "mp", "ctx"),
    )
    out_specs = P("section", "ctx", "mp")
    two = mesh.shape["ctx"] == 2 and mesh.shape["mp"] == 4
    return jax.shard_map(
        two_by_four if two else any_mesh, mesh=mesh, in_specs=in_specs, out_specs=out_specs, check_vma=False
    )
```

```python
import functools
import math

import jax
import jax.numpy as jnp
import ml_dtypes
import numpy as np
from jax import lax
from jax.experimental import pallas as pl
from jax.experimental.pallas import tpu as pltpu
from jax.sharding import PartitionSpec as P

F32 = jnp.float32
BF16 = jnp.bfloat16
EXTRA = 16
VMEM_LIMIT = 24 * 2**20
LANES = 256
WIDE = 512
CHUNKS = 2


def odd_tables(length):
    k = np.arange(length, dtype=np.int64)[:, None]
    n = np.arange(length, dtype=np.int64)[None, :]
    turn = ((2 * k + 1) * n) % (4 * length)
    angle = turn.astype(np.float64) * (math.pi / (2 * length))
    forward = np.concatenate([np.cos(angle), np.sin(angle)], axis=0)
    high = forward.astype(ml_dtypes.bfloat16)
    low = (forward - high.astype(np.float64)).astype(ml_dtypes.bfloat16)
    scale = np.float64(1.0 / length)
    back = forward.T * scale
    back_high = back.astype(ml_dtypes.bfloat16)
    back_low = (back - back_high.astype(np.float64)).astype(ml_dtypes.bfloat16)
    return high, low, back_high, back_low


def down(rows, by):
    index = lax.broadcasted_iota(jnp.int32, rows.shape, 0)
    return jnp.where(index >= by, pltpu.roll(rows, by, 0), 0.0)


def short_filtered(rows, taps):
    return taps[0:1] * rows + taps[1:2] * down(rows, 1) + taps[2:3] * down(rows, 2)


def span(index, size):
    return pl.ds(pl.multiple_of(index * size, size), size)


def mix_kernel(flip, place, key_ref, value_ref, taps_ref, out_ref):
    rows, width = out_ref.shape[0] - EXTRA, out_ref.shape[1]
    half = 1 - place[0] if flip else place[0]
    for lane in range(0, width, LANES):
        lanes = pl.ds(pl.multiple_of(half * width + lane, LANES), LANES)
        key = key_ref[0, :, lanes].astype(F32)
        value = value_ref[0, :, lanes].astype(F32)
        mixed = short_filtered(key, taps_ref[1, :, 0, lanes]) * short_filtered(value, taps_ref[2, :, 0, lanes])
        out_ref[:rows, lane : lane + LANES] = mixed.astype(BF16)
        edges = [key[:2], key[rows - 2 :], value[:2], value[rows - 2 :], jnp.zeros((EXTRA - 8, LANES), F32)]
        out_ref[rows:, lane : lane + LANES] = jnp.concatenate(edges, axis=0).astype(BF16)


def filter_kernel(place, own_ref, come_ref, high_ref, low_ref, spec_ref, whole):
    rows, width = come_ref.shape
    whole[span(place[0], rows), :] = own_ref[0, :, span(place[0], width)]
    whole[span(1 - place[0], rows), :] = come_ref[...]
    for lane in range(0, width, WIDE):
        data = whole[:, lane : lane + WIDE]
        spec_ref[:, lane : lane + WIDE] = jnp.dot(high_ref[...], data, preferred_element_type=F32) + jnp.dot(
            low_ref[...], data, preferred_element_type=F32
        )


def conv_kernel(
    place, own_ref, come_ref, taps_ref, spec_ref, high_ref, low_ref, back_high_ref, back_low_ref, out_ref, whole
):
    rows, width = own_ref.shape[0] - EXTRA, own_ref.shape[1]
    first = place[0] == 0
    whole[span(place[0], rows), :] = own_ref[:rows, :]
    whole[span(1 - place[0], rows), :] = come_ref[:rows, :]
    own_edge = own_ref[rows:, :].astype(F32)
    come_edge = come_ref[rows:, :].astype(F32)
    before = jnp.where(first, own_edge, come_edge)
    after = jnp.where(first, come_edge, own_edge)

    def edge_features(branch, base):
        taps = taps_ref[branch, :, 0, span(place[0], width)]
        older, old = before[base + 2 : base + 3], before[base + 3 : base + 4]
        new, newer = after[base : base + 1], after[base + 1 : base + 2]
        return (
            taps[0:1] * new + taps[1:2] * old + taps[2:3] * older,
            taps[0:1] * newer + taps[1:2] * new + taps[2:3] * old,
        )

    key_0, key_1 = edge_features(1, 0)
    value_0, value_1 = edge_features(2, 4)
    tile = whole[rows : rows + EXTRA, :].astype(F32)
    index = lax.broadcasted_iota(jnp.int32, tile.shape, 0)
    tile = jnp.where(index == 0, key_0 * value_0, jnp.where(index == 1, key_1 * value_1, tile))
    whole[rows : rows + EXTRA, :] = tile.astype(BF16)

    half = high_ref.shape[0] // 2
    for lane in range(0, width, WIDE):
        lanes = slice(lane, lane + WIDE)
        data = whole[:, lanes]
        spec = jnp.dot(high_ref[...], data, preferred_element_type=F32) + jnp.dot(
            low_ref[...], data, preferred_element_type=F32
        )
        cos_a, sin_a = spec[:half], spec[half:]
        cos_b, sin_b = spec_ref[:half, lanes], spec_ref[half:, lanes]
        product = jnp.concatenate([cos_a * cos_b - sin_a * sin_b, cos_a * sin_b + sin_a * cos_b], axis=0)
        product_high = product.astype(BF16)
        product_low = (product - product_high.astype(F32)).astype(BF16)
        out_ref[:, lanes] = (
            jnp.dot(back_high_ref[...], product_high, preferred_element_type=F32)
            + jnp.dot(back_low_ref[...], product_high, preferred_element_type=F32)
            + jnp.dot(back_high_ref[...], product_low, preferred_element_type=F32)
        )


def gate_kernel(place, own_ref, come_ref, taps_ref, conv_ref, here_ref, there_ref, whole):
    rows, width = come_ref.shape
    whole[span(place[0], rows), :] = own_ref[0, :, span(place[0], width)].astype(F32)
    whole[span(1 - place[0], rows), :] = come_ref[...].astype(F32)
    for lane in range(0, width, LANES):
        lanes = slice(lane, lane + LANES)
        taps = taps_ref[0, :, 0, pl.ds(pl.multiple_of(place[0] * width + lane, LANES), LANES)]
        whole[:, lanes] = short_filtered(whole[:, lanes], taps) * conv_ref[:, lanes]
    here_ref[...] = whole[span(place[0], rows), :].astype(BF16)
    there_ref[...] = whole[span(1 - place[0], rows), :].astype(BF16)


def project_kernel(place, same_ref, cross_ref, weight_ref, *out_refs):
    depth = same_ref.shape[1]
    columns = weight_ref.shape[2] // 2
    for flip, refs in ((1, out_refs[: len(out_refs) // 2]), (0, out_refs[len(out_refs) // 2 :])):
        block = lax.rem(place[1] + flip, 2)
        for tile in range(0, columns, WIDE):
            lanes = pl.ds(pl.multiple_of(block * columns + tile, WIDE), WIDE)
            value = jnp.dot(
                same_ref[...], weight_ref[0, span(place[0], depth), lanes], preferred_element_type=F32
            ) + jnp.dot(
                cross_ref[...], weight_ref[0, span(1 - place[0], depth), lanes], preferred_element_type=F32
            )
            start = 0
            for ref in refs:
                ref[:, tile : tile + WIDE] = value[start : start + ref.shape[0]].astype(ref.dtype)
                start += ref.shape[0]


def add_kernel(start, one_ref, two_ref, sum_ref):
    rows = slice(start, start + sum_ref.shape[0])
    sum_ref[...] = (one_ref[rows, :].astype(F32) + two_ref[...].astype(F32)).astype(BF16)


def last_kernel(place, own_keep_ref, own_near_ref, own_far_ref, *refs):
    out_ref, groups = refs[-1], len(refs) // 3
    size = refs[0].shape[0]

    @pl.when(place[2] == place[0])
    def _():
        total = own_keep_ref[...] + own_near_ref[...].astype(F32) + own_far_ref[...].astype(F32)
        out_ref[0] = total.astype(BF16)

    @pl.when(place[2] != place[0])
    def _():
        for c in range(groups):
            total = sum(ref[...].astype(F32) for ref in refs[3 * c : 3 * c + 3])
            out_ref[0, c * size : (c + 1) * size, :] = total.astype(BF16)


def local(kernel, out_shape, flops, *operands, scratch=()):
    moved = sum(math.prod(a.shape) * a.dtype.itemsize for a in list(operands) + list(out_shape))
    memory = [pltpu.SMEM if a.dtype == jnp.int32 else pltpu.VMEM for a in operands]
    return pl.pallas_call(
        kernel,
        out_shape=out_shape,
        in_specs=[pl.BlockSpec(memory_space=space) for space in memory],
        out_specs=[pl.BlockSpec(memory_space=pltpu.VMEM)] * len(out_shape),
        scratch_shapes=list(scratch),
        compiler_params=pltpu.CompilerParams(vmem_limit_bytes=VMEM_LIMIT),
        cost_estimate=pl.CostEstimate(flops=int(flops), bytes_accessed=int(moved), transcendentals=0),
    )(*operands)


def shape(dims, dtype):
    return jax.ShapeDtypeStruct(dims, dtype)


def two_by_four(query, key, value, filt, taps, weight):
    sections = lax.axis_size("section")
    rows, channels = query.shape[1:]
    width = channels // 2
    length = 2 * rows
    columns = weight.shape[2] // 2
    x = lax.axis_index("ctx")
    z = lax.axis_index("mp")
    taps = jnp.transpose(taps, (1, 2, 0, 3))
    place = jnp.stack([x, z % 2, z // 2]).astype(jnp.int32)
    high, low, back_high, back_low = (jnp.asarray(t) for t in odd_tables(length))

    swap = [(0, 1), (1, 0)]

    def other_half(array):
        return lax.dynamic_slice_in_dim(array[0], (1 - x) * width, width, axis=1)

    filt_come = lax.ppermute(other_half(filt), "ctx", swap)
    mixed = shape((rows + EXTRA, width), BF16)
    (mixed_send,) = local(functools.partial(mix_kernel, True), [mixed], 20 * rows * width, place, key, value, taps)
    mixed_come = lax.ppermute(mixed_send, "ctx", swap)
    query_come = lax.ppermute(other_half(query), "ctx", swap)
    (mixed_own,) = local(functools.partial(mix_kernel, False), [mixed], 20 * rows * width, place, key, value, taps)

    square = length * length * width
    half_bf16, half_f32 = pltpu.VMEM((length, width), BF16), pltpu.VMEM((length, width), F32)
    (spectrum,) = local(
        filter_kernel, [shape((2 * length, width), F32)], 8 * square, place, filt, filt_come, high, low,
        scratch=[half_bf16],
    )
    (convolved,) = local(
        conv_kernel, [shape((length, width), F32)], 20 * square, place, mixed_own, mixed_come, taps, spectrum,
        high, low, back_high, back_low, scratch=[half_bf16],
    )
    here, there = local(
        gate_kernel, [shape((rows, width), BF16)] * 2, 10 * length * width, place, query, query_come, taps, convolved,
        scratch=[half_f32],
    )

    def to_next(array, flip):
        pairs = [
            (s * 2 + c, (s + 1) % sections * 2 + (c + flip) % 2) for s in range(sections) for c in range(2)
        ]
        return lax.ppermute(array, ("section", "ctx"), pairs)

    cross_other, same_other = to_next(here, 1), to_next(there, 0)
    cross_own, same_own = to_next(there, 1), to_next(here, 0)

    chunk = rows // CHUNKS
    parts = [shape((chunk, columns), BF16)] * CHUNKS
    flops = 4 * rows * channels * columns
    pieces = local(project_kernel, parts + parts, flops, place, same_other, cross_other, weight)
    diagonal = [(c * 4 + m, (1 - c) * 4 + (m ^ 1)) for c in range(2) for m in range(4)]
    near = [(m, m ^ 1) for m in range(4)]
    far_own = [(c * 4 + m, c * 4 + (m ^ 2)) for c in range(2) for m in range(4) if m // 2 != c]
    far_cross = [(c * 4 + m, c * 4 + (m ^ 2)) for c in range(2) for m in range(4) if m // 2 == c]
    near_come, keep_come = [], []
    for c in range(CHUNKS):
        near_come.append(lax.ppermute(pieces[c], ("ctx", "mp"), diagonal))
        keep_come.append(lax.ppermute(pieces[CHUNKS + c], "ctx", swap))
    same_own, cross_own, pieces = lax.optimization_barrier((same_own, cross_own, pieces))
    pass_on, own_keep = local(
        project_kernel, [shape((rows, columns), BF16), shape((rows, columns), F32)], flops,
        place, same_own, cross_own, weight,
    )
    own_near = lax.ppermute(pass_on, "mp", near)
    (own_sum,) = local(functools.partial(add_kernel, 0), [shape((rows, columns), BF16)], rows * columns, own_keep, own_near)
    own_far = lax.ppermute(own_sum, ("ctx", "mp"), far_own)
    groups = []
    for near_part, keep_part in zip(near_come, keep_come):
        (part,) = local(functools.partial(add_kernel, 0), [shape((chunk, columns), BF16)], chunk * columns, near_part, keep_part)
        groups += [near_part, keep_part, lax.ppermute(part, ("ctx", "mp"), far_cross)]
    (result,) = local(
        last_kernel, [shape((1, rows, columns), BF16)], 3 * rows * columns, place, own_keep, own_near, own_far, *groups
    )
    return result


def from_behind(value, axis, by):
    count = lax.axis_size(axis)
    pairs = [(i, i + by) for i in range(count) if 0 <= i + by < count]
    return lax.ppermute(value, axis, pairs)


def from_behind_2(value, axis, by):
    count = lax.axis_size(axis)
    return lax.ppermute(value, axis, [(i, (i + by) % count) for i in range(count)])


def phase_table(left, right, modulus):
    product = left[:, None] * right[None, :] % modulus
    angle = product.astype(jnp.float32) * (2.0 * math.pi / modulus)
    return (jnp.cos(angle), jnp.sin(angle))


def contract(pattern, table, data):
    return jnp.einsum(pattern, table, data, precision=lax.Precision.HIGHEST)


def rotate(cos_tab, sin_tab, orient, pattern, real_part, imag_part):
    new_real = contract(pattern, cos_tab, real_part) - orient * contract(
        pattern, sin_tab, imag_part
    )
    new_imag = contract(pattern, cos_tab, imag_part) + orient * contract(
        pattern, sin_tab, real_part
    )
    return (new_real, new_imag)


def transform(real_part, imag_part, orient):
    length = real_part.shape[-2]
    outer_len = math.gcd(length, 2 ** ((length.bit_length() - 1) // 2))
    inner_len = length // outer_len
    leading = real_part.shape[:-2]
    channels = real_part.shape[-1]
    real_part = real_part.reshape(leading + (outer_len, inner_len, channels))
    imag_part = imag_part.reshape(leading + (outer_len, inner_len, channels))
    outer_ids = jnp.arange(outer_len, dtype=jnp.int32)
    inner_ids = jnp.arange(inner_len, dtype=jnp.int32)
    cos_outer, sin_outer = phase_table(outer_ids, outer_ids, outer_len)
    real_part, imag_part = rotate(
        cos_outer, sin_outer, orient, "kn,...nbc->...kbc", real_part, imag_part
    )
    cos_twist, sin_twist = phase_table(outer_ids, inner_ids, length)
    cos_twist = cos_twist[:, :, None]
    sin_twist = sin_twist[:, :, None]
    real_part, imag_part = (
        real_part * cos_twist - orient * imag_part * sin_twist,
        imag_part * cos_twist + orient * real_part * sin_twist,
    )
    cos_inner, sin_inner = phase_table(inner_ids, inner_ids, inner_len)
    real_part, imag_part = rotate(
        cos_inner, sin_inner, orient, "qb,...kbc->...qkc", real_part, imag_part
    )
    return (
        real_part.reshape(leading + (length, channels)),
        imag_part.reshape(leading + (length, channels)),
    )


def any_mesh(query_rows, key_rows, value_rows, long_filter, short_filter, next_weight):
    blocks = lax.axis_size("ctx")
    query_local = query_rows[0]
    key_local = key_rows[0]
    value_local = value_rows[0]
    tok_dev = query_local.shape[0]
    total = 2 * tok_dev * blocks
    stacked = jnp.stack([query_local[-2:], key_local[-2:], value_local[-2:]])
    carried = from_behind(stacked, "ctx", 1)
    taps = short_filter[0]

    def featurize(branch, current):
        extended = jnp.concatenate([carried[branch], current], axis=0).astype(jnp.float32)
        return (
            taps[branch, 0] * extended[2:]
            + taps[branch, 1] * extended[1:-1]
            + taps[branch, 2] * extended[:-2]
        )

    query_feat = featurize(0, query_local)
    mixed_input = featurize(1, key_local) * featurize(2, value_local)
    pair = jnp.stack([mixed_input, long_filter[0].astype(jnp.float32)])
    whole = lax.all_to_all(pair, "ctx", split_axis=2, concat_axis=1, tiled=True)
    padded = jnp.concatenate([whole, jnp.zeros_like(whole)], axis=1)
    spec_real, spec_imag = transform(padded, jnp.zeros_like(padded), -1.0)
    prod_real = spec_real[0] * spec_real[1] - spec_imag[0] * spec_imag[1]
    prod_imag = spec_real[0] * spec_imag[1] + spec_imag[0] * spec_real[1]
    conv_real, conv_imag = transform(prod_real, prod_imag, 1.0)
    values_out = conv_real[: tok_dev * blocks] / total
    convolved = lax.all_to_all(values_out, "ctx", split_axis=0, concat_axis=1, tiled=True)
    hyena_out = (query_feat * convolved).astype(jnp.bfloat16)
    incoming = from_behind_2(hyena_out, "section", 1)
    weight_local = next_weight[0]
    partial_value = jnp.dot(
        incoming,
        lax.all_gather(weight_local, "ctx", axis=1, tiled=True),
        preferred_element_type=jnp.float32,
    )
    summed = lax.psum_scatter(partial_value, "mp", scatter_dimension=1, tiled=True)
    return summed.astype(jnp.bfloat16)[None]


def solution(mesh):
    in_specs = (
        P("section", "ctx", "mp"),
        P("section", "ctx", "mp"),
        P("section", "ctx", "mp"),
        P("section", "ctx", "mp"),
        P("section", None, None, "mp"),
        P("section", "mp", "ctx"),
    )
    out_specs = P("section", "ctx", "mp")
    two = mesh.shape["ctx"] == 2 and mesh.shape["mp"] == 4
    return jax.shard_map(
        two_by_four if two else any_mesh, mesh=mesh, in_specs=in_specs, out_specs=out_specs, check_vma=False
    )
```

```python
import functools
import math

import jax
import jax.numpy as jnp
import ml_dtypes
import numpy as np
from jax import lax
from jax.experimental import pallas as pl
from jax.experimental.pallas import tpu as pltpu
from jax.sharding import PartitionSpec as P

F32 = jnp.float32
BF16 = jnp.bfloat16
EXTRA = 16
VMEM_LIMIT = 24 * 2**20
LANES = 256
WIDE = 512
OWN, CROSS = 2, 2
ORDER = [(0, 0), (1, 0), (0, 1), (1, 1)]


def odd_tables(length):
    k = np.arange(length, dtype=np.int64)[:, None]
    n = np.arange(length, dtype=np.int64)[None, :]
    turn = ((2 * k + 1) * n) % (4 * length)
    angle = turn.astype(np.float64) * (math.pi / (2 * length))
    forward = np.concatenate([np.cos(angle), np.sin(angle)], axis=0)
    high = forward.astype(ml_dtypes.bfloat16)
    low = (forward - high.astype(np.float64)).astype(ml_dtypes.bfloat16)
    scale = np.float64(1.0 / length)
    back = forward.T * scale
    back_high = back.astype(ml_dtypes.bfloat16)
    back_low = (back - back_high.astype(np.float64)).astype(ml_dtypes.bfloat16)
    return high, low, back_high, back_low


def down(rows, by):
    index = lax.broadcasted_iota(jnp.int32, rows.shape, 0)
    return jnp.where(index >= by, pltpu.roll(rows, by, 0), 0.0)


def short_filtered(rows, taps):
    return taps[0:1] * rows + taps[1:2] * down(rows, 1) + taps[2:3] * down(rows, 2)


def span(index, size):
    return pl.ds(pl.multiple_of(index * size, size), size)


def mix_kernel(flip, place, key_ref, value_ref, taps_ref, out_ref):
    rows, width = out_ref.shape[0] - EXTRA, out_ref.shape[1]
    half = 1 - place[0] if flip else place[0]
    for lane in range(0, width, LANES):
        lanes = pl.ds(pl.multiple_of(half * width + lane, LANES), LANES)
        key = key_ref[0, :, lanes].astype(F32)
        value = value_ref[0, :, lanes].astype(F32)
        mixed = short_filtered(key, taps_ref[1, :, 0, lanes]) * short_filtered(value, taps_ref[2, :, 0, lanes])
        out_ref[:rows, lane : lane + LANES] = mixed.astype(BF16)
        edges = [key[:2], key[rows - 2 :], value[:2], value[rows - 2 :], jnp.zeros((EXTRA - 8, LANES), F32)]
        out_ref[rows:, lane : lane + LANES] = jnp.concatenate(edges, axis=0).astype(BF16)


def filter_kernel(place, own_ref, come_ref, high_ref, low_ref, spec_ref, whole):
    rows, width = come_ref.shape
    whole[span(place[0], rows), :] = own_ref[0, :, span(place[0], width)]
    whole[span(1 - place[0], rows), :] = come_ref[...]
    for lane in range(0, width, WIDE):
        data = whole[:, lane : lane + WIDE]
        spec_ref[:, lane : lane + WIDE] = jnp.dot(high_ref[...], data, preferred_element_type=F32) + jnp.dot(
            low_ref[...], data, preferred_element_type=F32
        )


def conv_kernel(
    place, own_ref, come_ref, taps_ref, spec_ref, high_ref, low_ref, back_high_ref, back_low_ref, out_ref, whole
):
    rows, width = own_ref.shape[0] - EXTRA, own_ref.shape[1]
    first = place[0] == 0
    whole[span(place[0], rows), :] = own_ref[:rows, :]
    whole[span(1 - place[0], rows), :] = come_ref[:rows, :]
    own_edge = own_ref[rows:, :].astype(F32)
    come_edge = come_ref[rows:, :].astype(F32)
    before = jnp.where(first, own_edge, come_edge)
    after = jnp.where(first, come_edge, own_edge)

    def edge_features(branch, base):
        taps = taps_ref[branch, :, 0, span(place[0], width)]
        older, old = before[base + 2 : base + 3], before[base + 3 : base + 4]
        new, newer = after[base : base + 1], after[base + 1 : base + 2]
        return (
            taps[0:1] * new + taps[1:2] * old + taps[2:3] * older,
            taps[0:1] * newer + taps[1:2] * new + taps[2:3] * old,
        )

    key_0, key_1 = edge_features(1, 0)
    value_0, value_1 = edge_features(2, 4)
    tile = whole[rows : rows + EXTRA, :].astype(F32)
    index = lax.broadcasted_iota(jnp.int32, tile.shape, 0)
    tile = jnp.where(index == 0, key_0 * value_0, jnp.where(index == 1, key_1 * value_1, tile))
    whole[rows : rows + EXTRA, :] = tile.astype(BF16)

    half = high_ref.shape[0] // 2
    for lane in range(0, width, WIDE):
        lanes = slice(lane, lane + WIDE)
        data = whole[:, lanes]
        spec = jnp.dot(high_ref[...], data, preferred_element_type=F32) + jnp.dot(
            low_ref[...], data, preferred_element_type=F32
        )
        cos_a, sin_a = spec[:half], spec[half:]
        cos_b, sin_b = spec_ref[:half, lanes], spec_ref[half:, lanes]
        product = jnp.concatenate([cos_a * cos_b - sin_a * sin_b, cos_a * sin_b + sin_a * cos_b], axis=0)
        product_high = product.astype(BF16)
        product_low = (product - product_high.astype(F32)).astype(BF16)
        out_ref[:, lanes] = (
            jnp.dot(back_high_ref[...], product_high, preferred_element_type=F32)
            + jnp.dot(back_low_ref[...], product_high, preferred_element_type=F32)
            + jnp.dot(back_high_ref[...], product_low, preferred_element_type=F32)
        )


def gate_kernel(place, own_ref, come_ref, taps_ref, conv_ref, here_ref, there_ref, whole):
    rows, width = come_ref.shape
    whole[span(place[0], rows), :] = own_ref[0, :, span(place[0], width)].astype(F32)
    whole[span(1 - place[0], rows), :] = come_ref[...].astype(F32)
    for lane in range(0, width, LANES):
        lanes = slice(lane, lane + LANES)
        taps = taps_ref[0, :, 0, pl.ds(pl.multiple_of(place[0] * width + lane, LANES), LANES)]
        whole[:, lanes] = short_filtered(whole[:, lanes], taps) * conv_ref[:, lanes]
    here_ref[...] = whole[span(place[0], rows), :].astype(BF16)
    there_ref[...] = whole[span(1 - place[0], rows), :].astype(BF16)


def project_kernel(place, same_ref, cross_ref, weight_ref, *out_refs):
    depth = same_ref.shape[1]
    columns = weight_ref.shape[2] // 2
    for flip, refs in ((1, out_refs[: len(out_refs) // 2]), (0, out_refs[len(out_refs) // 2 :])):
        block = lax.rem(place[1] + flip, 2)
        for tile in range(0, columns, WIDE):
            lanes = pl.ds(pl.multiple_of(block * columns + tile, WIDE), WIDE)
            value = jnp.dot(
                same_ref[...], weight_ref[0, span(place[0], depth), lanes], preferred_element_type=F32
            ) + jnp.dot(
                cross_ref[...], weight_ref[0, span(1 - place[0], depth), lanes], preferred_element_type=F32
            )
            start = 0
            for ref in refs:
                ref[:, tile : tile + WIDE] = value[start : start + ref.shape[0]].astype(ref.dtype)
                start += ref.shape[0]


def add_kernel(one_ref, two_ref, sum_ref):
    sum_ref[...] = (one_ref[...].astype(F32) + two_ref[...].astype(F32)).astype(BF16)


def last_kernel(own, place, *refs):
    out_ref = refs[-1]
    for at_home, group in ((True, refs[: 3 * own]), (False, refs[3 * own : -1])):

        @pl.when((place[2] == place[0]) == at_home)
        def _():
            size = group[0].shape[0]
            for c in range(len(group) // 3):
                total = sum(ref[...].astype(F32) for ref in group[3 * c : 3 * c + 3])
                out_ref[0, c * size : (c + 1) * size, :] = total.astype(BF16)


def local(kernel, out_shape, flops, *operands, scratch=()):
    moved = sum(math.prod(a.shape) * a.dtype.itemsize for a in list(operands) + list(out_shape))
    memory = [pltpu.SMEM if a.dtype == jnp.int32 else pltpu.VMEM for a in operands]
    return pl.pallas_call(
        kernel,
        out_shape=out_shape,
        in_specs=[pl.BlockSpec(memory_space=space) for space in memory],
        out_specs=[pl.BlockSpec(memory_space=pltpu.VMEM)] * len(out_shape),
        scratch_shapes=list(scratch),
        compiler_params=pltpu.CompilerParams(vmem_limit_bytes=VMEM_LIMIT),
        cost_estimate=pl.CostEstimate(flops=int(flops), bytes_accessed=int(moved), transcendentals=0),
    )(*operands)


def shape(dims, dtype):
    return jax.ShapeDtypeStruct(dims, dtype)


def two_by_four(query, key, value, filt, taps, weight):
    sections = lax.axis_size("section")
    rows, channels = query.shape[1:]
    width = channels // 2
    length = 2 * rows
    columns = weight.shape[2] // 2
    x = lax.axis_index("ctx")
    z = lax.axis_index("mp")
    taps = jnp.transpose(taps, (1, 2, 0, 3))
    place = jnp.stack([x, z % 2, z // 2]).astype(jnp.int32)
    high, low, back_high, back_low = (jnp.asarray(t) for t in odd_tables(length))

    swap = [(0, 1), (1, 0)]

    def other_half(array):
        return lax.dynamic_slice_in_dim(array[0], (1 - x) * width, width, axis=1)

    filt_come = lax.ppermute(other_half(filt), "ctx", swap)
    mixed = shape((rows + EXTRA, width), BF16)
    (mixed_send,) = local(functools.partial(mix_kernel, True), [mixed], 20 * rows * width, place, key, value, taps)
    mixed_come = lax.ppermute(mixed_send, "ctx", swap)
    query_come = lax.ppermute(other_half(query), "ctx", swap)
    (mixed_own,) = local(functools.partial(mix_kernel, False), [mixed], 20 * rows * width, place, key, value, taps)

    square = length * length * width
    half_bf16, half_f32 = pltpu.VMEM((length, width), BF16), pltpu.VMEM((length, width), F32)
    (spectrum,) = local(
        filter_kernel, [shape((2 * length, width), F32)], 8 * square, place, filt, filt_come, high, low,
        scratch=[half_bf16],
    )
    (convolved,) = local(
        conv_kernel, [shape((length, width), F32)], 20 * square, place, mixed_own, mixed_come, taps, spectrum,
        high, low, back_high, back_low, scratch=[half_bf16],
    )
    here, there = local(
        gate_kernel, [shape((rows, width), BF16)] * 2, 10 * length * width, place, query, query_come, taps, convolved,
        scratch=[half_f32],
    )

    def to_next(array, flip):
        pairs = [
            (s * 2 + c, (s + 1) % sections * 2 + (c + flip) % 2) for s in range(sections) for c in range(2)
        ]
        return lax.ppermute(array, ("section", "ctx"), pairs)

    cross_own, same_own = to_next(there, 1), to_next(here, 0)
    cross_other, same_other = to_next(here, 1), to_next(there, 0)

    flops = 4 * rows * channels * columns
    diagonal = [(c * 4 + m, (1 - c) * 4 + (m ^ 1)) for c in range(2) for m in range(4)]
    near = [(m, m ^ 1) for m in range(4)]
    far_own = [(c * 4 + m, c * 4 + (m ^ 2)) for c in range(2) for m in range(4) if m // 2 != c]
    far_cross = [(c * 4 + m, c * 4 + (m ^ 2)) for c in range(2) for m in range(4) if m // 2 == c]

    def blocks(count, dtype):
        return [shape((rows // count, columns), dtype)] * count

    def add(one, two):
        return local(add_kernel, [shape(one.shape, BF16)], math.prod(one.shape), one, two)[0]

    owned = local(
        project_kernel, blocks(OWN, BF16) + blocks(OWN, F32), flops, place, same_own, cross_own, weight
    )
    same_other, cross_other, owned = lax.optimization_barrier((same_other, cross_other, owned))
    pieces = local(
        project_kernel, blocks(CROSS, BF16) + blocks(CROSS, BF16), flops, place, same_other, cross_other, weight
    )
    own_near = [lax.ppermute(piece, "mp", near) for piece in owned[:OWN]]
    near_come = [lax.ppermute(piece, ("ctx", "mp"), diagonal) for piece in pieces[:CROSS]]
    keep_come = [lax.ppermute(piece, "ctx", swap) for piece in pieces[CROSS:]]
    pairs = {0: list(zip(owned[OWN:], own_near)), 1: list(zip(near_come, keep_come))}
    held, sums = None, {}
    for role, c in ORDER:
        pair = pairs[role][c]
        if held is not None:
            pair = lax.optimization_barrier(pair + (held,))[:2]
        held = sums[role, c] = add(*pair)
    groups = []
    for role, count, far in ((0, OWN, far_own), (1, CROSS, far_cross)):
        for c in range(count):
            groups += [*pairs[role][c], lax.ppermute(sums[role, c], ("ctx", "mp"), far)]
    (result,) = local(
        functools.partial(last_kernel, OWN), [shape((1, rows, columns), BF16)], 3 * rows * columns, place, *groups
    )
    return result


def from_behind(value, axis, by):
    count = lax.axis_size(axis)
    pairs = [(i, i + by) for i in range(count) if 0 <= i + by < count]
    return lax.ppermute(value, axis, pairs)


def from_behind_2(value, axis, by):
    count = lax.axis_size(axis)
    return lax.ppermute(value, axis, [(i, (i + by) % count) for i in range(count)])


def phase_table(left, right, modulus):
    product = left[:, None] * right[None, :] % modulus
    angle = product.astype(jnp.float32) * (2.0 * math.pi / modulus)
    return (jnp.cos(angle), jnp.sin(angle))


def contract(pattern, table, data):
    return jnp.einsum(pattern, table, data, precision=lax.Precision.HIGHEST)


def rotate(cos_tab, sin_tab, orient, pattern, real_part, imag_part):
    new_real = contract(pattern, cos_tab, real_part) - orient * contract(
        pattern, sin_tab, imag_part
    )
    new_imag = contract(pattern, cos_tab, imag_part) + orient * contract(
        pattern, sin_tab, real_part
    )
    return (new_real, new_imag)


def transform(real_part, imag_part, orient):
    length = real_part.shape[-2]
    outer_len = math.gcd(length, 2 ** ((length.bit_length() - 1) // 2))
    inner_len = length // outer_len
    leading = real_part.shape[:-2]
    channels = real_part.shape[-1]
    real_part = real_part.reshape(leading + (outer_len, inner_len, channels))
    imag_part = imag_part.reshape(leading + (outer_len, inner_len, channels))
    outer_ids = jnp.arange(outer_len, dtype=jnp.int32)
    inner_ids = jnp.arange(inner_len, dtype=jnp.int32)
    cos_outer, sin_outer = phase_table(outer_ids, outer_ids, outer_len)
    real_part, imag_part = rotate(
        cos_outer, sin_outer, orient, "kn,...nbc->...kbc", real_part, imag_part
    )
    cos_twist, sin_twist = phase_table(outer_ids, inner_ids, length)
    cos_twist = cos_twist[:, :, None]
    sin_twist = sin_twist[:, :, None]
    real_part, imag_part = (
        real_part * cos_twist - orient * imag_part * sin_twist,
        imag_part * cos_twist + orient * real_part * sin_twist,
    )
    cos_inner, sin_inner = phase_table(inner_ids, inner_ids, inner_len)
    real_part, imag_part = rotate(
        cos_inner, sin_inner, orient, "qb,...kbc->...qkc", real_part, imag_part
    )
    return (
        real_part.reshape(leading + (length, channels)),
        imag_part.reshape(leading + (length, channels)),
    )


def any_mesh(query_rows, key_rows, value_rows, long_filter, short_filter, next_weight):
    blocks = lax.axis_size("ctx")
    query_local = query_rows[0]
    key_local = key_rows[0]
    value_local = value_rows[0]
    tok_dev = query_local.shape[0]
    total = 2 * tok_dev * blocks
    stacked = jnp.stack([query_local[-2:], key_local[-2:], value_local[-2:]])
    carried = from_behind(stacked, "ctx", 1)
    taps = short_filter[0]

    def featurize(branch, current):
        extended = jnp.concatenate([carried[branch], current], axis=0).astype(jnp.float32)
        return (
            taps[branch, 0] * extended[2:]
            + taps[branch, 1] * extended[1:-1]
            + taps[branch, 2] * extended[:-2]
        )

    query_feat = featurize(0, query_local)
    mixed_input = featurize(1, key_local) * featurize(2, value_local)
    pair = jnp.stack([mixed_input, long_filter[0].astype(jnp.float32)])
    whole = lax.all_to_all(pair, "ctx", split_axis=2, concat_axis=1, tiled=True)
    padded = jnp.concatenate([whole, jnp.zeros_like(whole)], axis=1)
    spec_real, spec_imag = transform(padded, jnp.zeros_like(padded), -1.0)
    prod_real = spec_real[0] * spec_real[1] - spec_imag[0] * spec_imag[1]
    prod_imag = spec_real[0] * spec_imag[1] + spec_imag[0] * spec_real[1]
    conv_real, conv_imag = transform(prod_real, prod_imag, 1.0)
    values_out = conv_real[: tok_dev * blocks] / total
    convolved = lax.all_to_all(values_out, "ctx", split_axis=0, concat_axis=1, tiled=True)
    hyena_out = (query_feat * convolved).astype(jnp.bfloat16)
    incoming = from_behind_2(hyena_out, "section", 1)
    weight_local = next_weight[0]
    partial_value = jnp.dot(
        incoming,
        lax.all_gather(weight_local, "ctx", axis=1, tiled=True),
        preferred_element_type=jnp.float32,
    )
    summed = lax.psum_scatter(partial_value, "mp", scatter_dimension=1, tiled=True)
    return summed.astype(jnp.bfloat16)[None]


def solution(mesh):
    in_specs = (
        P("section", "ctx", "mp"),
        P("section", "ctx", "mp"),
        P("section", "ctx", "mp"),
        P("section", "ctx", "mp"),
        P("section", None, None, "mp"),
        P("section", "mp", "ctx"),
    )
    out_specs = P("section", "ctx", "mp")
    two = mesh.shape["ctx"] == 2 and mesh.shape["mp"] == 4
    return jax.shard_map(
        two_by_four if two else any_mesh, mesh=mesh, in_specs=in_specs, out_specs=out_specs, check_vma=False
    )
```

```python
import functools
import math

import jax
import jax.numpy as jnp
import ml_dtypes
import numpy as np
from jax import lax
from jax.experimental import pallas as pl
from jax.experimental.pallas import tpu as pltpu
from jax.sharding import PartitionSpec as P

F32 = jnp.float32
BF16 = jnp.bfloat16
EXTRA = 16
VMEM_LIMIT = 24 * 2**20
LANES = 256
WIDE = 512
OWN, CROSS = 2, 2
ORDER = [(0, 0, None), (1, 0, None), (0, 1, (1, 0)), (1, 1, (0, 1))]


def odd_tables(length):
    k = np.arange(length, dtype=np.int64)[:, None]
    n = np.arange(length, dtype=np.int64)[None, :]
    turn = ((2 * k + 1) * n) % (4 * length)
    angle = turn.astype(np.float64) * (math.pi / (2 * length))
    forward = np.concatenate([np.cos(angle), np.sin(angle)], axis=0)
    high = forward.astype(ml_dtypes.bfloat16)
    low = (forward - high.astype(np.float64)).astype(ml_dtypes.bfloat16)
    scale = np.float64(1.0 / length)
    back = forward.T * scale
    back_high = back.astype(ml_dtypes.bfloat16)
    back_low = (back - back_high.astype(np.float64)).astype(ml_dtypes.bfloat16)
    return high, low, back_high, back_low


def down(rows, by):
    index = lax.broadcasted_iota(jnp.int32, rows.shape, 0)
    return jnp.where(index >= by, pltpu.roll(rows, by, 0), 0.0)


def short_filtered(rows, taps):
    return taps[0:1] * rows + taps[1:2] * down(rows, 1) + taps[2:3] * down(rows, 2)


def span(index, size):
    return pl.ds(pl.multiple_of(index * size, size), size)


def mix_kernel(flip, place, key_ref, value_ref, taps_ref, out_ref):
    rows, width = out_ref.shape[0] - EXTRA, out_ref.shape[1]
    half = 1 - place[0] if flip else place[0]
    for lane in range(0, width, LANES):
        lanes = pl.ds(pl.multiple_of(half * width + lane, LANES), LANES)
        key = key_ref[0, :, lanes].astype(F32)
        value = value_ref[0, :, lanes].astype(F32)
        mixed = short_filtered(key, taps_ref[1, :, 0, lanes]) * short_filtered(value, taps_ref[2, :, 0, lanes])
        out_ref[:rows, lane : lane + LANES] = mixed.astype(BF16)
        edges = [key[:2], key[rows - 2 :], value[:2], value[rows - 2 :], jnp.zeros((EXTRA - 8, LANES), F32)]
        out_ref[rows:, lane : lane + LANES] = jnp.concatenate(edges, axis=0).astype(BF16)


def filter_kernel(place, own_ref, come_ref, high_ref, low_ref, spec_ref, whole):
    rows, width = come_ref.shape
    whole[span(place[0], rows), :] = own_ref[0, :, span(place[0], width)]
    whole[span(1 - place[0], rows), :] = come_ref[...]
    for lane in range(0, width, WIDE):
        data = whole[:, lane : lane + WIDE]
        spec_ref[:, lane : lane + WIDE] = jnp.dot(high_ref[...], data, preferred_element_type=F32) + jnp.dot(
            low_ref[...], data, preferred_element_type=F32
        )


def conv_kernel(
    place, own_ref, come_ref, taps_ref, spec_ref, high_ref, low_ref, back_high_ref, back_low_ref, out_ref, whole
):
    rows, width = own_ref.shape[0] - EXTRA, own_ref.shape[1]
    first = place[0] == 0
    whole[span(place[0], rows), :] = own_ref[:rows, :]
    whole[span(1 - place[0], rows), :] = come_ref[:rows, :]
    own_edge = own_ref[rows:, :].astype(F32)
    come_edge = come_ref[rows:, :].astype(F32)
    before = jnp.where(first, own_edge, come_edge)
    after = jnp.where(first, come_edge, own_edge)

    def edge_features(branch, base):
        taps = taps_ref[branch, :, 0, span(place[0], width)]
        older, old = before[base + 2 : base + 3], before[base + 3 : base + 4]
        new, newer = after[base : base + 1], after[base + 1 : base + 2]
        return (
            taps[0:1] * new + taps[1:2] * old + taps[2:3] * older,
            taps[0:1] * newer + taps[1:2] * new + taps[2:3] * old,
        )

    key_0, key_1 = edge_features(1, 0)
    value_0, value_1 = edge_features(2, 4)
    tile = whole[rows : rows + EXTRA, :].astype(F32)
    index = lax.broadcasted_iota(jnp.int32, tile.shape, 0)
    tile = jnp.where(index == 0, key_0 * value_0, jnp.where(index == 1, key_1 * value_1, tile))
    whole[rows : rows + EXTRA, :] = tile.astype(BF16)

    half = high_ref.shape[0] // 2
    for lane in range(0, width, WIDE):
        lanes = slice(lane, lane + WIDE)
        data = whole[:, lanes]
        spec = jnp.dot(high_ref[...], data, preferred_element_type=F32) + jnp.dot(
            low_ref[...], data, preferred_element_type=F32
        )
        cos_a, sin_a = spec[:half], spec[half:]
        cos_b, sin_b = spec_ref[:half, lanes], spec_ref[half:, lanes]
        product = jnp.concatenate([cos_a * cos_b - sin_a * sin_b, cos_a * sin_b + sin_a * cos_b], axis=0)
        product_high = product.astype(BF16)
        product_low = (product - product_high.astype(F32)).astype(BF16)
        out_ref[:, lanes] = (
            jnp.dot(back_high_ref[...], product_high, preferred_element_type=F32)
            + jnp.dot(back_low_ref[...], product_high, preferred_element_type=F32)
            + jnp.dot(back_high_ref[...], product_low, preferred_element_type=F32)
        )


def gate_kernel(own, place, current_ref, previous_ref, taps_ref, conv_ref, out_ref):
    rows, width = out_ref.shape
    half = place[0] if own else 1 - place[0]
    for lane in range(0, width, LANES):
        mine = pl.ds(pl.multiple_of(place[0] * width + lane, LANES), LANES)
        rest = slice(lane, lane + LANES)
        taps = taps_ref[0, :, 0, mine]
        if own:
            current, before = current_ref[0, :, mine], previous_ref[rows - EXTRA :, rest]
        else:
            current, before = current_ref[:, rest], previous_ref[0, rows - EXTRA :, mine]
        current = current.astype(F32)
        before = jnp.where(half == 1, before.astype(F32), 0.0)
        old, older = before[EXTRA - 1 :], before[EXTRA - 2 : EXTRA - 1]
        index = lax.broadcasted_iota(jnp.int32, current.shape, 0)
        one = jnp.where(index == 0, old, pltpu.roll(current, 1, 0))
        two = jnp.where(index == 0, older, jnp.where(index == 1, old, pltpu.roll(current, 2, 0)))
        feature = taps[0:1] * current + taps[1:2] * one + taps[2:3] * two
        out_ref[:, rest] = (feature * conv_ref[span(half, rows), rest]).astype(BF16)


def project_kernel(place, same_ref, cross_ref, weight_ref, *out_refs):
    depth = same_ref.shape[1]
    columns = weight_ref.shape[2] // 2
    for flip, refs in ((1, out_refs[: len(out_refs) // 2]), (0, out_refs[len(out_refs) // 2 :])):
        block = lax.rem(place[1] + flip, 2)
        for tile in range(0, columns, WIDE):
            lanes = pl.ds(pl.multiple_of(block * columns + tile, WIDE), WIDE)
            value = jnp.dot(
                same_ref[...], weight_ref[0, span(place[0], depth), lanes], preferred_element_type=F32
            ) + jnp.dot(
                cross_ref[...], weight_ref[0, span(1 - place[0], depth), lanes], preferred_element_type=F32
            )
            start = 0
            for ref in refs:
                ref[:, tile : tile + WIDE] = value[start : start + ref.shape[0]].astype(ref.dtype)
                start += ref.shape[0]


def add_kernel(one_ref, two_ref, sum_ref):
    sum_ref[...] = (one_ref[...].astype(F32) + two_ref[...].astype(F32)).astype(BF16)


def last_kernel(own, place, *refs):
    out_ref = refs[-1]
    for at_home, group in ((True, refs[: 3 * own]), (False, refs[3 * own : -1])):

        @pl.when((place[2] == place[0]) == at_home)
        def _():
            size = group[0].shape[0]
            for c in range(len(group) // 3):
                total = sum(ref[...].astype(F32) for ref in group[3 * c : 3 * c + 3])
                out_ref[0, c * size : (c + 1) * size, :] = total.astype(BF16)


def local(kernel, out_shape, flops, *operands, scratch=()):
    moved = sum(math.prod(a.shape) * a.dtype.itemsize for a in list(operands) + list(out_shape))
    memory = [pltpu.SMEM if a.dtype == jnp.int32 else pltpu.VMEM for a in operands]
    return pl.pallas_call(
        kernel,
        out_shape=out_shape,
        in_specs=[pl.BlockSpec(memory_space=space) for space in memory],
        out_specs=[pl.BlockSpec(memory_space=pltpu.VMEM)] * len(out_shape),
        scratch_shapes=list(scratch),
        compiler_params=pltpu.CompilerParams(vmem_limit_bytes=VMEM_LIMIT),
        cost_estimate=pl.CostEstimate(flops=int(flops), bytes_accessed=int(moved), transcendentals=0),
    )(*operands)


def shape(dims, dtype):
    return jax.ShapeDtypeStruct(dims, dtype)


def two_by_four(query, key, value, filt, taps, weight):
    sections = lax.axis_size("section")
    rows, channels = query.shape[1:]
    width = channels // 2
    length = 2 * rows
    columns = weight.shape[2] // 2
    x = lax.axis_index("ctx")
    z = lax.axis_index("mp")
    taps = jnp.transpose(taps, (1, 2, 0, 3))
    place = jnp.stack([x, z % 2, z // 2]).astype(jnp.int32)
    high, low, back_high, back_low = (jnp.asarray(t) for t in odd_tables(length))

    swap = [(0, 1), (1, 0)]

    def other_half(array):
        return lax.dynamic_slice_in_dim(array[0], (1 - x) * width, width, axis=1)

    filt_come = lax.ppermute(other_half(filt), "ctx", swap)
    mixed = shape((rows + EXTRA, width), BF16)
    (mixed_send,) = local(functools.partial(mix_kernel, True), [mixed], 20 * rows * width, place, key, value, taps)
    mixed_come = lax.ppermute(mixed_send, "ctx", swap)
    query_come = lax.ppermute(other_half(query), "ctx", swap)
    (mixed_own,) = local(functools.partial(mix_kernel, False), [mixed], 20 * rows * width, place, key, value, taps)

    square = length * length * width
    half_bf16 = pltpu.VMEM((length, width), BF16)
    (spectrum,) = local(
        filter_kernel, [shape((2 * length, width), F32)], 8 * square, place, filt, filt_come, high, low,
        scratch=[half_bf16],
    )
    (convolved,) = local(
        conv_kernel, [shape((length, width), F32)], 20 * square, place, mixed_own, mixed_come, taps, spectrum,
        high, low, back_high, back_low, scratch=[half_bf16],
    )
    half = [shape((rows, width), BF16)]
    there = local(
        functools.partial(gate_kernel, False), half, 5 * length * width, place, query_come, query, taps, convolved
    )[0]
    here = local(
        functools.partial(gate_kernel, True), half, 5 * length * width, place, query, query_come, taps, convolved
    )[0]

    def to_next(array, flip):
        pairs = [
            (s * 2 + c, (s + 1) % sections * 2 + (c + flip) % 2) for s in range(sections) for c in range(2)
        ]
        return lax.ppermute(array, ("section", "ctx"), pairs)

    cross_own, same_own = to_next(there, 1), to_next(here, 0)
    cross_other, same_other = to_next(here, 1), to_next(there, 0)

    flops = 4 * rows * channels * columns
    diagonal = [(c * 4 + m, (1 - c) * 4 + (m ^ 1)) for c in range(2) for m in range(4)]
    near = [(m, m ^ 1) for m in range(4)]
    far_own = [(c * 4 + m, c * 4 + (m ^ 2)) for c in range(2) for m in range(4) if m // 2 != c]
    far_cross = [(c * 4 + m, c * 4 + (m ^ 2)) for c in range(2) for m in range(4) if m // 2 == c]

    def blocks(count, dtype):
        return [shape((rows // count, columns), dtype)] * count

    def add(one, two):
        return local(add_kernel, [shape(one.shape, BF16)], math.prod(one.shape), one, two)[0]

    owned = local(
        project_kernel, blocks(OWN, BF16) + blocks(OWN, F32), flops, place, same_own, cross_own, weight
    )
    same_other, cross_other, owned = lax.optimization_barrier((same_other, cross_other, owned))
    pieces = local(
        project_kernel, blocks(CROSS, BF16) + blocks(CROSS, BF16), flops, place, same_other, cross_other, weight
    )
    own_near = [lax.ppermute(piece, "mp", near) for piece in owned[:OWN]]
    near_come = [lax.ppermute(piece, ("ctx", "mp"), diagonal) for piece in pieces[:CROSS]]
    keep_come = [lax.ppermute(piece, "ctx", swap) for piece in pieces[CROSS:]]
    pairs = {0: list(zip(owned[OWN:], own_near)), 1: list(zip(near_come, keep_come))}
    sums = {}
    for role, c, after in ORDER:
        pair = pairs[role][c]
        if after is not None:
            pair = lax.optimization_barrier(pair + (sums[after],))[:2]
        sums[role, c] = add(*pair)
    groups = []
    for role, count, far in ((0, OWN, far_own), (1, CROSS, far_cross)):
        for c in range(count):
            groups += [*pairs[role][c], lax.ppermute(sums[role, c], ("ctx", "mp"), far)]
    (result,) = local(
        functools.partial(last_kernel, OWN), [shape((1, rows, columns), BF16)], 3 * rows * columns, place, *groups
    )
    return result


def from_behind(value, axis, by):
    count = lax.axis_size(axis)
    pairs = [(i, i + by) for i in range(count) if 0 <= i + by < count]
    return lax.ppermute(value, axis, pairs)


def from_behind_2(value, axis, by):
    count = lax.axis_size(axis)
    return lax.ppermute(value, axis, [(i, (i + by) % count) for i in range(count)])


def phase_table(left, right, modulus):
    product = left[:, None] * right[None, :] % modulus
    angle = product.astype(jnp.float32) * (2.0 * math.pi / modulus)
    return (jnp.cos(angle), jnp.sin(angle))


def contract(pattern, table, data):
    return jnp.einsum(pattern, table, data, precision=lax.Precision.HIGHEST)


def rotate(cos_tab, sin_tab, orient, pattern, real_part, imag_part):
    new_real = contract(pattern, cos_tab, real_part) - orient * contract(
        pattern, sin_tab, imag_part
    )
    new_imag = contract(pattern, cos_tab, imag_part) + orient * contract(
        pattern, sin_tab, real_part
    )
    return (new_real, new_imag)


def transform(real_part, imag_part, orient):
    length = real_part.shape[-2]
    outer_len = math.gcd(length, 2 ** ((length.bit_length() - 1) // 2))
    inner_len = length // outer_len
    leading = real_part.shape[:-2]
    channels = real_part.shape[-1]
    real_part = real_part.reshape(leading + (outer_len, inner_len, channels))
    imag_part = imag_part.reshape(leading + (outer_len, inner_len, channels))
    outer_ids = jnp.arange(outer_len, dtype=jnp.int32)
    inner_ids = jnp.arange(inner_len, dtype=jnp.int32)
    cos_outer, sin_outer = phase_table(outer_ids, outer_ids, outer_len)
    real_part, imag_part = rotate(
        cos_outer, sin_outer, orient, "kn,...nbc->...kbc", real_part, imag_part
    )
    cos_twist, sin_twist = phase_table(outer_ids, inner_ids, length)
    cos_twist = cos_twist[:, :, None]
    sin_twist = sin_twist[:, :, None]
    real_part, imag_part = (
        real_part * cos_twist - orient * imag_part * sin_twist,
        imag_part * cos_twist + orient * real_part * sin_twist,
    )
    cos_inner, sin_inner = phase_table(inner_ids, inner_ids, inner_len)
    real_part, imag_part = rotate(
        cos_inner, sin_inner, orient, "qb,...kbc->...qkc", real_part, imag_part
    )
    return (
        real_part.reshape(leading + (length, channels)),
        imag_part.reshape(leading + (length, channels)),
    )


def any_mesh(query_rows, key_rows, value_rows, long_filter, short_filter, next_weight):
    blocks = lax.axis_size("ctx")
    query_local = query_rows[0]
    key_local = key_rows[0]
    value_local = value_rows[0]
    tok_dev = query_local.shape[0]
    total = 2 * tok_dev * blocks
    stacked = jnp.stack([query_local[-2:], key_local[-2:], value_local[-2:]])
    carried = from_behind(stacked, "ctx", 1)
    taps = short_filter[0]

    def featurize(branch, current):
        extended = jnp.concatenate([carried[branch], current], axis=0).astype(jnp.float32)
        return (
            taps[branch, 0] * extended[2:]
            + taps[branch, 1] * extended[1:-1]
            + taps[branch, 2] * extended[:-2]
        )

    query_feat = featurize(0, query_local)
    mixed_input = featurize(1, key_local) * featurize(2, value_local)
    pair = jnp.stack([mixed_input, long_filter[0].astype(jnp.float32)])
    whole = lax.all_to_all(pair, "ctx", split_axis=2, concat_axis=1, tiled=True)
    padded = jnp.concatenate([whole, jnp.zeros_like(whole)], axis=1)
    spec_real, spec_imag = transform(padded, jnp.zeros_like(padded), -1.0)
    prod_real = spec_real[0] * spec_real[1] - spec_imag[0] * spec_imag[1]
    prod_imag = spec_real[0] * spec_imag[1] + spec_imag[0] * spec_real[1]
    conv_real, conv_imag = transform(prod_real, prod_imag, 1.0)
    values_out = conv_real[: tok_dev * blocks] / total
    convolved = lax.all_to_all(values_out, "ctx", split_axis=0, concat_axis=1, tiled=True)
    hyena_out = (query_feat * convolved).astype(jnp.bfloat16)
    incoming = from_behind_2(hyena_out, "section", 1)
    weight_local = next_weight[0]
    partial_value = jnp.dot(
        incoming,
        lax.all_gather(weight_local, "ctx", axis=1, tiled=True),
        preferred_element_type=jnp.float32,
    )
    summed = lax.psum_scatter(partial_value, "mp", scatter_dimension=1, tiled=True)
    return summed.astype(jnp.bfloat16)[None]


def solution(mesh):
    in_specs = (
        P("section", "ctx", "mp"),
        P("section", "ctx", "mp"),
        P("section", "ctx", "mp"),
        P("section", "ctx", "mp"),
        P("section", None, None, "mp"),
        P("section", "mp", "ctx"),
    )
    out_specs = P("section", "ctx", "mp")
    two = mesh.shape["ctx"] == 2 and mesh.shape["mp"] == 4
    return jax.shard_map(
        two_by_four if two else any_mesh, mesh=mesh, in_specs=in_specs, out_specs=out_specs, check_vma=False
    )
```

```python
import functools
import math

import jax
import jax.numpy as jnp
import ml_dtypes
import numpy as np
from jax import lax
from jax.experimental import pallas as pl
from jax.experimental.pallas import tpu as pltpu
from jax.sharding import PartitionSpec as P

F32 = jnp.float32
BF16 = jnp.bfloat16
EXTRA = 16
VMEM_LIMIT = 24 * 2**20
LANES = 512
WIDE = 512
OWN, CROSS = 2, 2
ORDER = [(0, 0, None), (1, 0, None), (0, 1, (1, 0)), (1, 1, (0, 1))]


def odd_tables(length):
    k = np.arange(length, dtype=np.int64)[:, None]
    n = np.arange(length, dtype=np.int64)[None, :]
    turn = ((2 * k + 1) * n) % (4 * length)
    angle = turn.astype(np.float64) * (math.pi / (2 * length))
    forward = np.concatenate([np.cos(angle), np.sin(angle)], axis=0)
    high = forward.astype(ml_dtypes.bfloat16)
    low = (forward - high.astype(np.float64)).astype(ml_dtypes.bfloat16)
    scale = np.float64(1.0 / length)
    back = forward.T * scale
    back_high = back.astype(ml_dtypes.bfloat16)
    back_low = (back - back_high.astype(np.float64)).astype(ml_dtypes.bfloat16)
    return high, low, back_high, back_low


def down(rows, by):
    index = lax.broadcasted_iota(jnp.int32, rows.shape, 0)
    return jnp.where(index >= by, pltpu.roll(rows, by, 0), 0.0)


def short_filtered(rows, taps):
    return taps[0:1] * rows + taps[1:2] * down(rows, 1) + taps[2:3] * down(rows, 2)


def span(index, size):
    return pl.ds(pl.multiple_of(index * size, size), size)


def mix_kernel(flip, place, key_ref, value_ref, taps_ref, out_ref):
    rows, width = out_ref.shape[0] - EXTRA, out_ref.shape[1]
    half = 1 - place[0] if flip else place[0]
    for lane in range(0, width, LANES):
        lanes = pl.ds(pl.multiple_of(half * width + lane, LANES), LANES)
        key = key_ref[0, :, lanes].astype(F32)
        value = value_ref[0, :, lanes].astype(F32)
        mixed = short_filtered(key, taps_ref[1, :, 0, lanes]) * short_filtered(value, taps_ref[2, :, 0, lanes])
        out_ref[:rows, lane : lane + LANES] = mixed.astype(BF16)
        edges = [key[:2], key[rows - 2 :], value[:2], value[rows - 2 :], jnp.zeros((EXTRA - 8, LANES), F32)]
        out_ref[rows:, lane : lane + LANES] = jnp.concatenate(edges, axis=0).astype(BF16)


def filter_kernel(place, own_ref, come_ref, high_ref, low_ref, spec_ref, whole):
    rows, width = come_ref.shape
    whole[span(place[0], rows), :] = own_ref[0, :, span(place[0], width)]
    whole[span(1 - place[0], rows), :] = come_ref[...]
    for lane in range(0, width, WIDE):
        data = whole[:, lane : lane + WIDE]
        spec_ref[:, lane : lane + WIDE] = jnp.dot(high_ref[...], data, preferred_element_type=F32) + jnp.dot(
            low_ref[...], data, preferred_element_type=F32
        )


def conv_kernel(
    place, own_ref, come_ref, taps_ref, spec_ref, high_ref, low_ref, back_high_ref, back_low_ref, out_ref, whole
):
    rows, width = own_ref.shape[0] - EXTRA, own_ref.shape[1]
    first = place[0] == 0
    whole[span(place[0], rows), :] = own_ref[:rows, :]
    whole[span(1 - place[0], rows), :] = come_ref[:rows, :]
    own_edge = own_ref[rows:, :].astype(F32)
    come_edge = come_ref[rows:, :].astype(F32)
    before = jnp.where(first, own_edge, come_edge)
    after = jnp.where(first, come_edge, own_edge)

    def edge_features(branch, base):
        taps = taps_ref[branch, :, 0, span(place[0], width)]
        older, old = before[base + 2 : base + 3], before[base + 3 : base + 4]
        new, newer = after[base : base + 1], after[base + 1 : base + 2]
        return (
            taps[0:1] * new + taps[1:2] * old + taps[2:3] * older,
            taps[0:1] * newer + taps[1:2] * new + taps[2:3] * old,
        )

    key_0, key_1 = edge_features(1, 0)
    value_0, value_1 = edge_features(2, 4)
    tile = whole[rows : rows + EXTRA, :].astype(F32)
    index = lax.broadcasted_iota(jnp.int32, tile.shape, 0)
    tile = jnp.where(index == 0, key_0 * value_0, jnp.where(index == 1, key_1 * value_1, tile))
    whole[rows : rows + EXTRA, :] = tile.astype(BF16)

    half = high_ref.shape[0] // 2
    for lane in range(0, width, WIDE):
        lanes = slice(lane, lane + WIDE)
        data = whole[:, lanes]
        spec = jnp.dot(high_ref[...], data, preferred_element_type=F32) + jnp.dot(
            low_ref[...], data, preferred_element_type=F32
        )
        cos_a, sin_a = spec[:half], spec[half:]
        cos_b, sin_b = spec_ref[:half, lanes], spec_ref[half:, lanes]
        product = jnp.concatenate([cos_a * cos_b - sin_a * sin_b, cos_a * sin_b + sin_a * cos_b], axis=0)
        product_high = product.astype(BF16)
        product_low = (product - product_high.astype(F32)).astype(BF16)
        out_ref[:, lanes] = (
            jnp.dot(back_high_ref[...], product_high, preferred_element_type=F32)
            + jnp.dot(back_low_ref[...], product_high, preferred_element_type=F32)
            + jnp.dot(back_high_ref[...], product_low, preferred_element_type=F32)
        )


def gate_kernel(own, place, current_ref, previous_ref, taps_ref, conv_ref, out_ref):
    rows, width = out_ref.shape
    half = place[0] if own else 1 - place[0]
    for lane in range(0, width, LANES):
        mine = pl.ds(pl.multiple_of(place[0] * width + lane, LANES), LANES)
        rest = slice(lane, lane + LANES)
        taps = taps_ref[0, :, 0, mine]
        if own:
            current, before = current_ref[0, :, mine], previous_ref[rows - EXTRA :, rest]
        else:
            current, before = current_ref[:, rest], previous_ref[0, rows - EXTRA :, mine]
        current = current.astype(F32)
        before = jnp.where(half == 1, before.astype(F32), 0.0)
        old, older = before[EXTRA - 1 :], before[EXTRA - 2 : EXTRA - 1]
        index = lax.broadcasted_iota(jnp.int32, current.shape, 0)
        one = jnp.where(index == 0, old, pltpu.roll(current, 1, 0))
        two = jnp.where(index == 0, older, jnp.where(index == 1, old, pltpu.roll(current, 2, 0)))
        feature = taps[0:1] * current + taps[1:2] * one + taps[2:3] * two
        out_ref[:, rest] = (feature * conv_ref[span(half, rows), rest]).astype(BF16)


def project_kernel(place, same_ref, cross_ref, weight_ref, *out_refs):
    depth = same_ref.shape[1]
    columns = weight_ref.shape[2] // 2
    for flip, refs in ((1, out_refs[: len(out_refs) // 2]), (0, out_refs[len(out_refs) // 2 :])):
        block = lax.rem(place[1] + flip, 2)
        for tile in range(0, columns, WIDE):
            lanes = pl.ds(pl.multiple_of(block * columns + tile, WIDE), WIDE)
            value = jnp.dot(
                same_ref[...], weight_ref[0, span(place[0], depth), lanes], preferred_element_type=F32
            ) + jnp.dot(
                cross_ref[...], weight_ref[0, span(1 - place[0], depth), lanes], preferred_element_type=F32
            )
            start = 0
            for ref in refs:
                ref[:, tile : tile + WIDE] = value[start : start + ref.shape[0]].astype(ref.dtype)
                start += ref.shape[0]


def add_kernel(one_ref, two_ref, sum_ref):
    sum_ref[...] = (one_ref[...].astype(F32) + two_ref[...].astype(F32)).astype(BF16)


def last_kernel(own, place, *refs):
    out_ref = refs[-1]
    for at_home, group in ((True, refs[: 3 * own]), (False, refs[3 * own : -1])):

        @pl.when((place[2] == place[0]) == at_home)
        def _():
            size = group[0].shape[0]
            for c in range(len(group) // 3):
                total = sum(ref[...].astype(F32) for ref in group[3 * c : 3 * c + 3])
                out_ref[0, c * size : (c + 1) * size, :] = total.astype(BF16)


def local(kernel, out_shape, flops, *operands, scratch=()):
    moved = sum(math.prod(a.shape) * a.dtype.itemsize for a in list(operands) + list(out_shape))
    memory = [pltpu.SMEM if a.dtype == jnp.int32 else pltpu.VMEM for a in operands]
    return pl.pallas_call(
        kernel,
        out_shape=out_shape,
        in_specs=[pl.BlockSpec(memory_space=space) for space in memory],
        out_specs=[pl.BlockSpec(memory_space=pltpu.VMEM)] * len(out_shape),
        scratch_shapes=list(scratch),
        compiler_params=pltpu.CompilerParams(vmem_limit_bytes=VMEM_LIMIT),
        cost_estimate=pl.CostEstimate(flops=int(flops), bytes_accessed=int(moved), transcendentals=0),
    )(*operands)


def shape(dims, dtype):
    return jax.ShapeDtypeStruct(dims, dtype)


def two_by_four(query, key, value, filt, taps, weight):
    sections = lax.axis_size("section")
    rows, channels = query.shape[1:]
    width = channels // 2
    length = 2 * rows
    columns = weight.shape[2] // 2
    x = lax.axis_index("ctx")
    z = lax.axis_index("mp")
    taps = jnp.transpose(taps, (1, 2, 0, 3))
    place = jnp.stack([x, z % 2, z // 2]).astype(jnp.int32)
    high, low, back_high, back_low = (jnp.asarray(t) for t in odd_tables(length))

    swap = [(0, 1), (1, 0)]

    def other_half(array):
        return lax.dynamic_slice_in_dim(array[0], (1 - x) * width, width, axis=1)

    filt_come = lax.ppermute(other_half(filt), "ctx", swap)
    mixed = shape((rows + EXTRA, width), BF16)
    (mixed_send,) = local(functools.partial(mix_kernel, True), [mixed], 20 * rows * width, place, key, value, taps)
    mixed_come = lax.ppermute(mixed_send, "ctx", swap)
    query_come = lax.ppermute(other_half(query), "ctx", swap)
    (mixed_own,) = local(functools.partial(mix_kernel, False), [mixed], 20 * rows * width, place, key, value, taps)

    square = length * length * width
    half_bf16 = pltpu.VMEM((length, width), BF16)
    (spectrum,) = local(
        filter_kernel, [shape((2 * length, width), F32)], 8 * square, place, filt, filt_come, high, low,
        scratch=[half_bf16],
    )
    (convolved,) = local(
        conv_kernel, [shape((length, width), F32)], 20 * square, place, mixed_own, mixed_come, taps, spectrum,
        high, low, back_high, back_low, scratch=[half_bf16],
    )
    half = [shape((rows, width), BF16)]
    there = local(
        functools.partial(gate_kernel, False), half, 5 * length * width, place, query_come, query, taps, convolved
    )[0]
    here = local(
        functools.partial(gate_kernel, True), half, 5 * length * width, place, query, query_come, taps, convolved
    )[0]

    def to_next(array, flip):
        pairs = [
            (s * 2 + c, (s + 1) % sections * 2 + (c + flip) % 2) for s in range(sections) for c in range(2)
        ]
        return lax.ppermute(array, ("section", "ctx"), pairs)

    cross_own, same_own = to_next(there, 1), to_next(here, 0)
    cross_other, same_other = to_next(here, 1), to_next(there, 0)

    flops = 4 * rows * channels * columns
    diagonal = [(c * 4 + m, (1 - c) * 4 + (m ^ 1)) for c in range(2) for m in range(4)]
    near = [(m, m ^ 1) for m in range(4)]
    far_own = [(c * 4 + m, c * 4 + (m ^ 2)) for c in range(2) for m in range(4) if m // 2 != c]
    far_cross = [(c * 4 + m, c * 4 + (m ^ 2)) for c in range(2) for m in range(4) if m // 2 == c]

    def blocks(count, dtype):
        return [shape((rows // count, columns), dtype)] * count

    def add(one, two):
        return local(add_kernel, [shape(one.shape, BF16)], math.prod(one.shape), one, two)[0]

    owned = local(
        project_kernel, blocks(OWN, BF16) + blocks(OWN, F32), flops, place, same_own, cross_own, weight
    )
    same_other, cross_other, owned = lax.optimization_barrier((same_other, cross_other, owned))
    pieces = local(
        project_kernel, blocks(CROSS, BF16) + blocks(CROSS, BF16), flops, place, same_other, cross_other, weight
    )
    own_near = [lax.ppermute(piece, "mp", near) for piece in owned[:OWN]]
    near_come = [lax.ppermute(piece, ("ctx", "mp"), diagonal) for piece in pieces[:CROSS]]
    keep_come = [lax.ppermute(piece, "ctx", swap) for piece in pieces[CROSS:]]
    pairs = {0: list(zip(owned[OWN:], own_near)), 1: list(zip(near_come, keep_come))}
    sums = {}
    for role, c, after in ORDER:
        pair = pairs[role][c]
        if after is not None:
            pair = lax.optimization_barrier(pair + (sums[after],))[:2]
        sums[role, c] = add(*pair)
    groups = []
    for role, count, far in ((0, OWN, far_own), (1, CROSS, far_cross)):
        for c in range(count):
            groups += [*pairs[role][c], lax.ppermute(sums[role, c], ("ctx", "mp"), far)]
    (result,) = local(
        functools.partial(last_kernel, OWN), [shape((1, rows, columns), BF16)], 3 * rows * columns, place, *groups
    )
    return result


def from_behind(value, axis, by):
    count = lax.axis_size(axis)
    pairs = [(i, i + by) for i in range(count) if 0 <= i + by < count]
    return lax.ppermute(value, axis, pairs)


def from_behind_2(value, axis, by):
    count = lax.axis_size(axis)
    return lax.ppermute(value, axis, [(i, (i + by) % count) for i in range(count)])


def phase_table(left, right, modulus):
    product = left[:, None] * right[None, :] % modulus
    angle = product.astype(jnp.float32) * (2.0 * math.pi / modulus)
    return (jnp.cos(angle), jnp.sin(angle))


def contract(pattern, table, data):
    return jnp.einsum(pattern, table, data, precision=lax.Precision.HIGHEST)


def rotate(cos_tab, sin_tab, orient, pattern, real_part, imag_part):
    new_real = contract(pattern, cos_tab, real_part) - orient * contract(
        pattern, sin_tab, imag_part
    )
    new_imag = contract(pattern, cos_tab, imag_part) + orient * contract(
        pattern, sin_tab, real_part
    )
    return (new_real, new_imag)


def transform(real_part, imag_part, orient):
    length = real_part.shape[-2]
    outer_len = math.gcd(length, 2 ** ((length.bit_length() - 1) // 2))
    inner_len = length // outer_len
    leading = real_part.shape[:-2]
    channels = real_part.shape[-1]
    real_part = real_part.reshape(leading + (outer_len, inner_len, channels))
    imag_part = imag_part.reshape(leading + (outer_len, inner_len, channels))
    outer_ids = jnp.arange(outer_len, dtype=jnp.int32)
    inner_ids = jnp.arange(inner_len, dtype=jnp.int32)
    cos_outer, sin_outer = phase_table(outer_ids, outer_ids, outer_len)
    real_part, imag_part = rotate(
        cos_outer, sin_outer, orient, "kn,...nbc->...kbc", real_part, imag_part
    )
    cos_twist, sin_twist = phase_table(outer_ids, inner_ids, length)
    cos_twist = cos_twist[:, :, None]
    sin_twist = sin_twist[:, :, None]
    real_part, imag_part = (
        real_part * cos_twist - orient * imag_part * sin_twist,
        imag_part * cos_twist + orient * real_part * sin_twist,
    )
    cos_inner, sin_inner = phase_table(inner_ids, inner_ids, inner_len)
    real_part, imag_part = rotate(
        cos_inner, sin_inner, orient, "qb,...kbc->...qkc", real_part, imag_part
    )
    return (
        real_part.reshape(leading + (length, channels)),
        imag_part.reshape(leading + (length, channels)),
    )


def any_mesh(query_rows, key_rows, value_rows, long_filter, short_filter, next_weight):
    blocks = lax.axis_size("ctx")
    query_local = query_rows[0]
    key_local = key_rows[0]
    value_local = value_rows[0]
    tok_dev = query_local.shape[0]
    total = 2 * tok_dev * blocks
    stacked = jnp.stack([query_local[-2:], key_local[-2:], value_local[-2:]])
    carried = from_behind(stacked, "ctx", 1)
    taps = short_filter[0]

    def featurize(branch, current):
        extended = jnp.concatenate([carried[branch], current], axis=0).astype(jnp.float32)
        return (
            taps[branch, 0] * extended[2:]
            + taps[branch, 1] * extended[1:-1]
            + taps[branch, 2] * extended[:-2]
        )

    query_feat = featurize(0, query_local)
    mixed_input = featurize(1, key_local) * featurize(2, value_local)
    pair = jnp.stack([mixed_input, long_filter[0].astype(jnp.float32)])
    whole = lax.all_to_all(pair, "ctx", split_axis=2, concat_axis=1, tiled=True)
    padded = jnp.concatenate([whole, jnp.zeros_like(whole)], axis=1)
    spec_real, spec_imag = transform(padded, jnp.zeros_like(padded), -1.0)
    prod_real = spec_real[0] * spec_real[1] - spec_imag[0] * spec_imag[1]
    prod_imag = spec_real[0] * spec_imag[1] + spec_imag[0] * spec_real[1]
    conv_real, conv_imag = transform(prod_real, prod_imag, 1.0)
    values_out = conv_real[: tok_dev * blocks] / total
    convolved = lax.all_to_all(values_out, "ctx", split_axis=0, concat_axis=1, tiled=True)
    hyena_out = (query_feat * convolved).astype(jnp.bfloat16)
    incoming = from_behind_2(hyena_out, "section", 1)
    weight_local = next_weight[0]
    partial_value = jnp.dot(
        incoming,
        lax.all_gather(weight_local, "ctx", axis=1, tiled=True),
        preferred_element_type=jnp.float32,
    )
    summed = lax.psum_scatter(partial_value, "mp", scatter_dimension=1, tiled=True)
    return summed.astype(jnp.bfloat16)[None]


def solution(mesh):
    in_specs = (
        P("section", "ctx", "mp"),
        P("section", "ctx", "mp"),
        P("section", "ctx", "mp"),
        P("section", "ctx", "mp"),
        P("section", None, None, "mp"),
        P("section", "mp", "ctx"),
    )
    out_specs = P("section", "ctx", "mp")
    two = mesh.shape["ctx"] == 2 and mesh.shape["mp"] == 4
    return jax.shard_map(
        two_by_four if two else any_mesh, mesh=mesh, in_specs=in_specs, out_specs=out_specs, check_vma=False
    )
```

```python
import functools
import math

import jax
import jax.numpy as jnp
import ml_dtypes
import numpy as np
from jax import lax
from jax.experimental import pallas as pl
from jax.experimental.pallas import tpu as pltpu
from jax.sharding import PartitionSpec as P

F32 = jnp.float32
BF16 = jnp.bfloat16
EXTRA = 16
VMEM_LIMIT = 24 * 2**20
LANES = 256
WIDE = 512
OWN, CROSS = 2, 2
ORDER = [(0, 0, None), (1, 0, None), (0, 1, (1, 0)), (1, 1, None)]


def odd_tables(length):
    k = np.arange(length, dtype=np.int64)[:, None]
    n = np.arange(length, dtype=np.int64)[None, :]
    turn = ((2 * k + 1) * n) % (4 * length)
    angle = turn.astype(np.float64) * (math.pi / (2 * length))
    forward = np.concatenate([np.cos(angle), np.sin(angle)], axis=0)
    high = forward.astype(ml_dtypes.bfloat16)
    low = (forward - high.astype(np.float64)).astype(ml_dtypes.bfloat16)
    scale = np.float64(1.0 / length)
    back = forward.T * scale
    back_high = back.astype(ml_dtypes.bfloat16)
    back_low = (back - back_high.astype(np.float64)).astype(ml_dtypes.bfloat16)
    return high, low, back_high, back_low


def down(rows, by):
    index = lax.broadcasted_iota(jnp.int32, rows.shape, 0)
    return jnp.where(index >= by, pltpu.roll(rows, by, 0), 0.0)


def short_filtered(rows, taps):
    return taps[0:1] * rows + taps[1:2] * down(rows, 1) + taps[2:3] * down(rows, 2)


def span(index, size):
    return pl.ds(pl.multiple_of(index * size, size), size)


def mix_kernel(flip, place, key_ref, value_ref, taps_ref, out_ref):
    rows, width = out_ref.shape[0] - EXTRA, out_ref.shape[1]
    half = 1 - place[0] if flip else place[0]
    for lane in range(0, width, LANES):
        lanes = pl.ds(pl.multiple_of(half * width + lane, LANES), LANES)
        key = key_ref[0, :, lanes].astype(F32)
        value = value_ref[0, :, lanes].astype(F32)
        mixed = short_filtered(key, taps_ref[1, :, 0, lanes]) * short_filtered(value, taps_ref[2, :, 0, lanes])
        out_ref[:rows, lane : lane + LANES] = mixed.astype(BF16)
        edges = [key[:2], key[rows - 2 :], value[:2], value[rows - 2 :], jnp.zeros((EXTRA - 8, LANES), F32)]
        out_ref[rows:, lane : lane + LANES] = jnp.concatenate(edges, axis=0).astype(BF16)


def filter_kernel(place, own_ref, come_ref, high_ref, low_ref, spec_ref, whole):
    rows, width = come_ref.shape
    whole[span(place[0], rows), :] = own_ref[0, :, span(place[0], width)]
    whole[span(1 - place[0], rows), :] = come_ref[...]
    for lane in range(0, width, WIDE):
        data = whole[:, lane : lane + WIDE]
        spec_ref[:, lane : lane + WIDE] = jnp.dot(high_ref[...], data, preferred_element_type=F32) + jnp.dot(
            low_ref[...], data, preferred_element_type=F32
        )


def conv_kernel(
    place, own_ref, come_ref, taps_ref, spec_ref, high_ref, low_ref, back_high_ref, back_low_ref, out_ref, whole
):
    rows, width = own_ref.shape[0] - EXTRA, own_ref.shape[1]
    first = place[0] == 0
    whole[span(place[0], rows), :] = own_ref[:rows, :]
    whole[span(1 - place[0], rows), :] = come_ref[:rows, :]
    own_edge = own_ref[rows:, :].astype(F32)
    come_edge = come_ref[rows:, :].astype(F32)
    before = jnp.where(first, own_edge, come_edge)
    after = jnp.where(first, come_edge, own_edge)

    def edge_features(branch, base):
        taps = taps_ref[branch, :, 0, span(place[0], width)]
        older, old = before[base + 2 : base + 3], before[base + 3 : base + 4]
        new, newer = after[base : base + 1], after[base + 1 : base + 2]
        return (
            taps[0:1] * new + taps[1:2] * old + taps[2:3] * older,
            taps[0:1] * newer + taps[1:2] * new + taps[2:3] * old,
        )

    key_0, key_1 = edge_features(1, 0)
    value_0, value_1 = edge_features(2, 4)
    tile = whole[rows : rows + EXTRA, :].astype(F32)
    index = lax.broadcasted_iota(jnp.int32, tile.shape, 0)
    tile = jnp.where(index == 0, key_0 * value_0, jnp.where(index == 1, key_1 * value_1, tile))
    whole[rows : rows + EXTRA, :] = tile.astype(BF16)

    half = high_ref.shape[0] // 2
    for lane in range(0, width, WIDE):
        lanes = slice(lane, lane + WIDE)
        data = whole[:, lanes]
        spec = jnp.dot(high_ref[...], data, preferred_element_type=F32) + jnp.dot(
            low_ref[...], data, preferred_element_type=F32
        )
        cos_a, sin_a = spec[:half], spec[half:]
        cos_b, sin_b = spec_ref[:half, lanes], spec_ref[half:, lanes]
        product = jnp.concatenate([cos_a * cos_b - sin_a * sin_b, cos_a * sin_b + sin_a * cos_b], axis=0)
        product_high = product.astype(BF16)
        product_low = (product - product_high.astype(F32)).astype(BF16)
        out_ref[:, lanes] = (
            jnp.dot(back_high_ref[...], product_high, preferred_element_type=F32)
            + jnp.dot(back_low_ref[...], product_high, preferred_element_type=F32)
            + jnp.dot(back_high_ref[...], product_low, preferred_element_type=F32)
        )


def gate_kernel(own, place, current_ref, previous_ref, taps_ref, conv_ref, out_ref):
    rows, width = out_ref.shape
    half = place[0] if own else 1 - place[0]
    for lane in range(0, width, LANES):
        mine = pl.ds(pl.multiple_of(place[0] * width + lane, LANES), LANES)
        rest = slice(lane, lane + LANES)
        taps = taps_ref[0, :, 0, mine]
        if own:
            current, before = current_ref[0, :, mine], previous_ref[rows - EXTRA :, rest]
        else:
            current, before = current_ref[:, rest], previous_ref[0, rows - EXTRA :, mine]
        current = current.astype(F32)
        before = jnp.where(half == 1, before.astype(F32), 0.0)
        old, older = before[EXTRA - 1 :], before[EXTRA - 2 : EXTRA - 1]
        index = lax.broadcasted_iota(jnp.int32, current.shape, 0)
        one = jnp.where(index == 0, old, pltpu.roll(current, 1, 0))
        two = jnp.where(index == 0, older, jnp.where(index == 1, old, pltpu.roll(current, 2, 0)))
        feature = taps[0:1] * current + taps[1:2] * one + taps[2:3] * two
        out_ref[:, rest] = (feature * conv_ref[span(half, rows), rest]).astype(BF16)


def project_kernel(place, same_ref, cross_ref, weight_ref, *out_refs):
    depth = same_ref.shape[1]
    columns = weight_ref.shape[2] // 2
    for flip, refs in ((1, out_refs[: len(out_refs) // 2]), (0, out_refs[len(out_refs) // 2 :])):
        block = lax.rem(place[1] + flip, 2)
        for tile in range(0, columns, WIDE):
            lanes = pl.ds(pl.multiple_of(block * columns + tile, WIDE), WIDE)
            value = jnp.dot(
                same_ref[...], weight_ref[0, span(place[0], depth), lanes], preferred_element_type=F32
            ) + jnp.dot(
                cross_ref[...], weight_ref[0, span(1 - place[0], depth), lanes], preferred_element_type=F32
            )
            start = 0
            for ref in refs:
                ref[:, tile : tile + WIDE] = value[start : start + ref.shape[0]].astype(ref.dtype)
                start += ref.shape[0]


def add_kernel(one_ref, two_ref, sum_ref):
    sum_ref[...] = (one_ref[...].astype(F32) + two_ref[...].astype(F32)).astype(BF16)


def last_kernel(own, place, *refs):
    out_ref = refs[-1]
    for at_home, group in ((True, refs[: 3 * own]), (False, refs[3 * own : -1])):

        @pl.when((place[2] == place[0]) == at_home)
        def _():
            size = group[0].shape[0]
            for c in range(len(group) // 3):
                total = sum(ref[...].astype(F32) for ref in group[3 * c : 3 * c + 3])
                out_ref[0, c * size : (c + 1) * size, :] = total.astype(BF16)


def local(kernel, out_shape, flops, *operands, scratch=()):
    moved = sum(math.prod(a.shape) * a.dtype.itemsize for a in list(operands) + list(out_shape))
    memory = [pltpu.SMEM if a.dtype == jnp.int32 else pltpu.VMEM for a in operands]
    return pl.pallas_call(
        kernel,
        out_shape=out_shape,
        in_specs=[pl.BlockSpec(memory_space=space) for space in memory],
        out_specs=[pl.BlockSpec(memory_space=pltpu.VMEM)] * len(out_shape),
        scratch_shapes=list(scratch),
        compiler_params=pltpu.CompilerParams(vmem_limit_bytes=VMEM_LIMIT),
        cost_estimate=pl.CostEstimate(flops=int(flops), bytes_accessed=int(moved), transcendentals=0),
    )(*operands)


def shape(dims, dtype):
    return jax.ShapeDtypeStruct(dims, dtype)


def two_by_four(query, key, value, filt, taps, weight):
    sections = lax.axis_size("section")
    rows, channels = query.shape[1:]
    width = channels // 2
    length = 2 * rows
    columns = weight.shape[2] // 2
    x = lax.axis_index("ctx")
    z = lax.axis_index("mp")
    taps = jnp.transpose(taps, (1, 2, 0, 3))
    place = jnp.stack([x, z % 2, z // 2]).astype(jnp.int32)
    high, low, back_high, back_low = (jnp.asarray(t) for t in odd_tables(length))

    swap = [(0, 1), (1, 0)]

    def other_half(array):
        return lax.dynamic_slice_in_dim(array[0], (1 - x) * width, width, axis=1)

    filt_come = lax.ppermute(other_half(filt), "ctx", swap)
    mixed = shape((rows + EXTRA, width), BF16)
    (mixed_send,) = local(functools.partial(mix_kernel, True), [mixed], 20 * rows * width, place, key, value, taps)
    mixed_come = lax.ppermute(mixed_send, "ctx", swap)
    query_come = lax.ppermute(other_half(query), "ctx", swap)
    (mixed_own,) = local(functools.partial(mix_kernel, False), [mixed], 20 * rows * width, place, key, value, taps)

    square = length * length * width
    half_bf16 = pltpu.VMEM((length, width), BF16)
    (spectrum,) = local(
        filter_kernel, [shape((2 * length, width), F32)], 8 * square, place, filt, filt_come, high, low,
        scratch=[half_bf16],
    )
    (convolved,) = local(
        conv_kernel, [shape((length, width), F32)], 20 * square, place, mixed_own, mixed_come, taps, spectrum,
        high, low, back_high, back_low, scratch=[half_bf16],
    )
    half = [shape((rows, width), BF16)]
    there = local(
        functools.partial(gate_kernel, False), half, 5 * length * width, place, query_come, query, taps, convolved
    )[0]
    here = local(
        functools.partial(gate_kernel, True), half, 5 * length * width, place, query, query_come, taps, convolved
    )[0]

    def to_next(array, flip):
        pairs = [
            (s * 2 + c, (s + 1) % sections * 2 + (c + flip) % 2) for s in range(sections) for c in range(2)
        ]
        return lax.ppermute(array, ("section", "ctx"), pairs)

    cross_own, same_own = to_next(there, 1), to_next(here, 0)
    cross_other, same_other = to_next(here, 1), to_next(there, 0)

    flops = 4 * rows * channels * columns
    diagonal = [(c * 4 + m, (1 - c) * 4 + (m ^ 1)) for c in range(2) for m in range(4)]
    near = [(m, m ^ 1) for m in range(4)]
    far_own = [(c * 4 + m, c * 4 + (m ^ 2)) for c in range(2) for m in range(4) if m // 2 != c]
    far_cross = [(c * 4 + m, c * 4 + (m ^ 2)) for c in range(2) for m in range(4) if m // 2 == c]

    def blocks(count, dtype):
        return [shape((rows // count, columns), dtype)] * count

    def add(one, two):
        return local(add_kernel, [shape(one.shape, BF16)], math.prod(one.shape), one, two)[0]

    owned = local(
        project_kernel, blocks(OWN, BF16) + blocks(OWN, F32), flops, place, same_own, cross_own, weight
    )
    same_other, cross_other, owned = lax.optimization_barrier((same_other, cross_other, owned))
    pieces = local(
        project_kernel, blocks(CROSS, BF16) + blocks(CROSS, BF16), flops, place, same_other, cross_other, weight
    )
    own_near = [lax.ppermute(piece, "mp", near) for piece in owned[:OWN]]
    near_come = [lax.ppermute(piece, ("ctx", "mp"), diagonal) for piece in pieces[:CROSS]]
    keep_come = [lax.ppermute(piece, "ctx", swap) for piece in pieces[CROSS:]]
    pairs = {0: list(zip(owned[OWN:], own_near)), 1: list(zip(near_come, keep_come))}
    sums = {}
    for role, c, after in ORDER:
        pair = pairs[role][c]
        if after is not None:
            pair = lax.optimization_barrier(pair + (sums[after],))[:2]
        sums[role, c] = add(*pair)
    groups = []
    for role, count, far in ((0, OWN, far_own), (1, CROSS, far_cross)):
        for c in range(count):
            groups += [*pairs[role][c], lax.ppermute(sums[role, c], ("ctx", "mp"), far)]
    (result,) = local(
        functools.partial(last_kernel, OWN), [shape((1, rows, columns), BF16)], 3 * rows * columns, place, *groups
    )
    return result


def from_behind(value, axis, by):
    count = lax.axis_size(axis)
    pairs = [(i, i + by) for i in range(count) if 0 <= i + by < count]
    return lax.ppermute(value, axis, pairs)


def from_behind_2(value, axis, by):
    count = lax.axis_size(axis)
    return lax.ppermute(value, axis, [(i, (i + by) % count) for i in range(count)])


def phase_table(left, right, modulus):
    product = left[:, None] * right[None, :] % modulus
    angle = product.astype(jnp.float32) * (2.0 * math.pi / modulus)
    return (jnp.cos(angle), jnp.sin(angle))


def contract(pattern, table, data):
    return jnp.einsum(pattern, table, data, precision=lax.Precision.HIGHEST)


def rotate(cos_tab, sin_tab, orient, pattern, real_part, imag_part):
    new_real = contract(pattern, cos_tab, real_part) - orient * contract(
        pattern, sin_tab, imag_part
    )
    new_imag = contract(pattern, cos_tab, imag_part) + orient * contract(
        pattern, sin_tab, real_part
    )
    return (new_real, new_imag)


def transform(real_part, imag_part, orient):
    length = real_part.shape[-2]
    outer_len = math.gcd(length, 2 ** ((length.bit_length() - 1) // 2))
    inner_len = length // outer_len
    leading = real_part.shape[:-2]
    channels = real_part.shape[-1]
    real_part = real_part.reshape(leading + (outer_len, inner_len, channels))
    imag_part = imag_part.reshape(leading + (outer_len, inner_len, channels))
    outer_ids = jnp.arange(outer_len, dtype=jnp.int32)
    inner_ids = jnp.arange(inner_len, dtype=jnp.int32)
    cos_outer, sin_outer = phase_table(outer_ids, outer_ids, outer_len)
    real_part, imag_part = rotate(
        cos_outer, sin_outer, orient, "kn,...nbc->...kbc", real_part, imag_part
    )
    cos_twist, sin_twist = phase_table(outer_ids, inner_ids, length)
    cos_twist = cos_twist[:, :, None]
    sin_twist = sin_twist[:, :, None]
    real_part, imag_part = (
        real_part * cos_twist - orient * imag_part * sin_twist,
        imag_part * cos_twist + orient * real_part * sin_twist,
    )
    cos_inner, sin_inner = phase_table(inner_ids, inner_ids, inner_len)
    real_part, imag_part = rotate(
        cos_inner, sin_inner, orient, "qb,...kbc->...qkc", real_part, imag_part
    )
    return (
        real_part.reshape(leading + (length, channels)),
        imag_part.reshape(leading + (length, channels)),
    )


def any_mesh(query_rows, key_rows, value_rows, long_filter, short_filter, next_weight):
    blocks = lax.axis_size("ctx")
    query_local = query_rows[0]
    key_local = key_rows[0]
    value_local = value_rows[0]
    tok_dev = query_local.shape[0]
    total = 2 * tok_dev * blocks
    stacked = jnp.stack([query_local[-2:], key_local[-2:], value_local[-2:]])
    carried = from_behind(stacked, "ctx", 1)
    taps = short_filter[0]

    def featurize(branch, current):
        extended = jnp.concatenate([carried[branch], current], axis=0).astype(jnp.float32)
        return (
            taps[branch, 0] * extended[2:]
            + taps[branch, 1] * extended[1:-1]
            + taps[branch, 2] * extended[:-2]
        )

    query_feat = featurize(0, query_local)
    mixed_input = featurize(1, key_local) * featurize(2, value_local)
    pair = jnp.stack([mixed_input, long_filter[0].astype(jnp.float32)])
    whole = lax.all_to_all(pair, "ctx", split_axis=2, concat_axis=1, tiled=True)
    padded = jnp.concatenate([whole, jnp.zeros_like(whole)], axis=1)
    spec_real, spec_imag = transform(padded, jnp.zeros_like(padded), -1.0)
    prod_real = spec_real[0] * spec_real[1] - spec_imag[0] * spec_imag[1]
    prod_imag = spec_real[0] * spec_imag[1] + spec_imag[0] * spec_real[1]
    conv_real, conv_imag = transform(prod_real, prod_imag, 1.0)
    values_out = conv_real[: tok_dev * blocks] / total
    convolved = lax.all_to_all(values_out, "ctx", split_axis=0, concat_axis=1, tiled=True)
    hyena_out = (query_feat * convolved).astype(jnp.bfloat16)
    incoming = from_behind_2(hyena_out, "section", 1)
    weight_local = next_weight[0]
    partial_value = jnp.dot(
        incoming,
        lax.all_gather(weight_local, "ctx", axis=1, tiled=True),
        preferred_element_type=jnp.float32,
    )
    summed = lax.psum_scatter(partial_value, "mp", scatter_dimension=1, tiled=True)
    return summed.astype(jnp.bfloat16)[None]


def solution(mesh):
    in_specs = (
        P("section", "ctx", "mp"),
        P("section", "ctx", "mp"),
        P("section", "ctx", "mp"),
        P("section", "ctx", "mp"),
        P("section", None, None, "mp"),
        P("section", "mp", "ctx"),
    )
    out_specs = P("section", "ctx", "mp")
    two = mesh.shape["ctx"] == 2 and mesh.shape["mp"] == 4
    return jax.shard_map(
        two_by_four if two else any_mesh, mesh=mesh, in_specs=in_specs, out_specs=out_specs, check_vma=False
    )
```
